128 devices in a mesh: tile: 16 (over z_hi, y, core), chan: 8 (over z_lo, x).
Axes of the slice: x: 4, y: 4, z: 4 (z_hi: 2, z_lo: 2; z = z_hi * 2 + z_lo), core: 2. Of those that a mesh axis runs over, the one named last changes fastest.
Arguments:
- features: bfloat16 [2, 96, 144, 2048], P(None, 'tile', 'chan'), may hold values from -6 to 6
- atrous_weight: bfloat16 [3, 3, 3, 2048, 256], P(None, None, None, 'tile', 'chan'), may hold values from -0.046875 to 0.046875
- point_weight: bfloat16 [2048, 256], P('tile', 'chan'), may hold values from -0.125 to 0.125
- branch_shift: float32 [4, 256], P(None, 'chan'), may hold values from -3 to 3
- proj_weight: bfloat16 [1024, 256], replicated, may hold values from -0.25 to 0.25
- class_weight: bfloat16 [256, 3], replicated, may hold values from -0.75 to 0.75
- labels: int32 [2, 96, 144], P(None, 'tile', 'chan'), may hold values from 0 to 2
Outputs:
- projected: bfloat16 [2, 96, 144, 256], P(None, 'tile', 'chan')
- pixel_loss: float32 [2, 96, 144], P(None, 'tile', 'chan')
The draws below stay inside these ranges and needn't reach their ends.
All inputs are finite; a program needn't handle non-finite values.
Results may differ from the reference program's by a relative error of at most 0.0049.
Values may be sent and summed in bfloat16 or wider, within the bound.
No kernel may reach another device: no remote copies, remote signals or barrier semaphores. Data moves between devices by JAX's collectives and lax.ppermute only.
A program may use at most 320 MiB of HBM per device.

```python
import jax
import jax.numpy as jnp
from jax import lax

C = 2048
A = 256
H = 96
W = 144
B = 2


def set_ends(drawn, own_key, least, top_value):
    longest = drawn.shape.index(max(drawn.shape))
    spots = []
    for shift in (0, 1):
        where = [jax.random.randint(jax.random.fold_in(own_key, axis), (), 0, length) for axis, length in enumerate(drawn.shape)]
        where[longest] = (where[longest] + shift) % drawn.shape[longest]
        spots.append(tuple(where))
    return drawn.at[spots[0]].set(least).at[spots[1]].set(top_value)


def shard_levels(own_key, extent, cuts, low, largest):
    def one(position, blocks):
        steps = jax.random.uniform(jax.random.fold_in(jax.random.fold_in(own_key, 6), position), (blocks,), jnp.float32, low / len(cuts), largest / len(cuts))
        return jnp.repeat(jnp.exp(steps), extent[position] // blocks).reshape((-1,) + (1,) * (len(extent) - position - 1))

    loudness = one(*cuts[0])
    for cut in cuts[1:]:
        loudness = loudness * one(*cut)
    return loudness


def scatter_about(key, shape, spread, limit, cuts=(), held_as=jnp.bfloat16):
    entries = jax.random.normal(key, shape, jnp.float32) * spread
    if len(cuts) > 0:
        entries = shard_levels(key, shape, cuts, -0.22, 0.18) * entries
    return jnp.clip(entries, min=-limit, max=limit).astype(held_as)


def setup_inputs(seed: int = 0) -> dict:
    keys = jax.random.split(jax.random.key(seed), 8)
    features = scatter_about(keys[0], (B, H, W, C), 1.0, 6.0, ((1, 16), (2, 8)))
    atrous_weight = scatter_about(keys[1], (3, 3, 3, C, A), (9 * C) ** -0.5, 0.046875, ((3, 16), (4, 8)))
    point_weight = scatter_about(keys[2], (C, A), C ** -0.5, 0.125, ((0, 16), (1, 8)))
    branch_shift = scatter_about(keys[3], (4, A), 0.5, 3.0, ((1, 8),), jnp.float32)
    proj_weight = scatter_about(keys[4], (4 * A, A), (2 * A) ** -0.5, 0.25)
    class_weight = scatter_about(keys[5], (A, 3), (A // 4) ** -0.5, 0.75)
    labels = set_ends(jax.random.randint(keys[6], (B, H, W), 0, 3), jax.random.fold_in(keys[6], 1), 0, 2).astype(jnp.int32)
    return dict(features=features, atrous_weight=atrous_weight, point_weight=point_weight, branch_shift=branch_shift, proj_weight=proj_weight, class_weight=class_weight, labels=labels)


def reference(features, atrous_weight, point_weight, branch_shift, proj_weight, class_weight, labels):
    pieces = [jnp.dot(features.reshape(-1, C), point_weight, preferred_element_type=jnp.float32).reshape(B, H, W, A)]
    for index, spacing in enumerate((12, 24, 36)):
        result = lax.conv_general_dilated(features, atrous_weight[index], (1, 1), ((spacing, spacing), (spacing, spacing)), rhs_dilation=(spacing, spacing), dimension_numbers=("NHWC", "HWIO", "NHWC"), preferred_element_type=jnp.float32)
        pieces.append(result)
    branches = jnp.concatenate(pieces, axis=-1) + branch_shift.reshape(-1)
    pyramid = jax.nn.relu(branches).astype(jnp.bfloat16)
    mixed = jnp.dot(pyramid.reshape(-1, 4 * A), proj_weight, preferred_element_type=jnp.float32)
    projected = jax.nn.relu(mixed).astype(jnp.bfloat16)
    logits = jnp.dot(projected, class_weight, preferred_element_type=jnp.float32)
    total = jnp.log(jnp.sum(jnp.exp(logits), axis=-1))
    chosen = jnp.sum(jnp.where(labels.reshape(-1, 1) == jnp.arange(3, dtype=jnp.int32), logits, 0.0), axis=-1)
    pixel_loss = (total - chosen).reshape(B, H, W)
    return projected.reshape(B, H, W, A), pixel_loss
```

```python
import jax
import jax.numpy as jnp
import numpy as np
from jax import lax
from jax.experimental import pallas as pl
from jax.experimental.pallas import tpu as pltpu
from jax.sharding import Mesh, PartitionSpec as P

ROWS = 32
GRID = 224
BF = jnp.bfloat16
F32 = jnp.float32
MIB = 1024 * 1024


def _message_row(i, t, c):
    return i * 9 + t * 3 + c


def _pack_matrix():
    m = np.zeros((256, 216), np.float32)
    for xq in range(4):
        for h in range(2):
            for i in range(3):
                for t in range(3):
                    for c in range(3):
                        row = (xq % 2) * 3 + i
                        col = 3 * (2 * t + h) + c
                        m[(xq * 2 + h) * ROWS + _message_row(i, t, c), (row * 18 + col) * 2 + xq // 2] = 1
    return m


def _unpack_matrices():
    by_cols = np.zeros((216, 256), np.float32)
    by_samples = np.zeros((216, 256), np.float32)
    for h in range(2):
        for xq in range(4):
            for i in range(3):
                for t in range(3):
                    for c in range(3):
                        row = (xq % 2) * 3 + i
                        col = 3 * (2 * t + h) + c
                        b = xq // 2
                        src = (h * 4 + xq) * ROWS + _message_row(i, t, c)
                        by_cols[(row * 18 + col) * 2 + b, src] = 1
                        by_samples[(row * 2 + b) * 18 + col, src] = 1
    return by_cols, by_samples


def _shift_matrices():
    m = np.zeros((7, GRID, 256), np.float32)
    for dc in range(-3, 4):
        for i in range(3):
            for gc in range(12):
                for u in range(6):
                    if 0 <= gc + dc < 12:
                        q = 2 * (gc + dc) + u // 3
                        m[dc + 3, (i * 12 + gc) * 6 + u, (q // 3) * ROWS + _message_row(i, q % 3, u % 3)] = 1
    return m


TAPS = (
    [(3, -1, 0), (2, -1, 0), (1, -1, 0), (0, 0, 0), (1, 0, 0), (2, 0, 0), (3, 0, 0), (1, 1, 0), (2, 1, 0), (3, 1, 0)]
    + [(d, a, c) for c in (-1, 1) for d in (1, 2, 3) for a in (-1, 0, 1)]
)


def _pack_kernel(p_ref, f_ref, out_ref):
    p = p_ref[...]
    for y in range(4):
        for z in range(2):
            part = f_ref[:, z * 1024 + y * 256 : z * 1024 + (y + 1) * 256]
            rows = jnp.dot(p, part, preferred_element_type=F32).astype(BF)
            for xq in range(4):
                for h in range(2):
                    piece = rows[(xq * 2 + h) * ROWS : (xq * 2 + h + 1) * ROWS]
                    for zl in range(2):
                        out_ref[((h * 4 + y) * 2 + zl) * 4 + xq, :, z * 256 : (z + 1) * 256] = piece


def _conv_kernel(where_ref, raw_ref, s_ref, st_ref, own_ref, other_ref, out_ref, xs, wt, sh, acc, sems):
    x, core, zh, first = where_ref[0], where_ref[1], where_ref[2], where_ref[3]
    copies = []
    for k in range(4):
        xo = lax.rem(x + k, 4)
        for z in range(2):
            for o, ref in enumerate((own_ref, other_ref)):
                slab = lax.rem(zh + z, 2) * 2 + lax.rem(core + o, 2)
                copies.append(
                    pltpu.make_async_copy(
                        ref.at[k, z, pl.ds(0, 28)],
                        wt.at[:, xo, :, pl.ds(pl.multiple_of(slab * 128, 128), 128)],
                        sems.at[len(copies)],
                    )
                )
        copies.append(pltpu.make_async_copy(own_ref.at[k, 0, 28], sh.at[xo], sems.at[len(copies)]))
    for copy in copies:
        copy.start()

    def spread(g, _):
        raw = raw_ref[pl.ds(g * 8, 8)].reshape(256, 512)
        for dc in range(7):
            xs[dc, g] = jnp.dot(s_ref[dc], raw, preferred_element_type=F32).astype(BF)
        return 0

    lax.fori_loop(0, 8, spread, 0)
    for copy in copies:
        copy.wait()

    lane = lax.broadcasted_iota(jnp.int32, (1, 128), 1)
    shifts = []
    for b in range(4):
        line = jnp.zeros((1, 128), F32)
        for xo in range(4):
            terms = sh[xo].astype(F32)
            whole = terms[0:1] + terms[1:2] + terms[2:3]
            if xo != b:
                whole = pltpu.roll(whole, ((xo - b) * 32) % 128, 1)
            line = jnp.where((lane >= xo * 32) & (lane < xo * 32 + 32), whole, line)
        shifts.append(jnp.where(first == 0, line, 0.0))
    for b in range(4):
        acc[b] = jnp.broadcast_to(shifts[b].reshape(1, 1, 128), (8, GRID, 128))

    def apply(s, dc, start, stop):
        t = start
        while t < stop:
            n = min(2, stop - t)
            w = wt[t : t + n].reshape(n * 128, 512)
            y = lax.dot_general(xs[dc + 3, s], w, (((1,), (1,)), ((), ())), preferred_element_type=F32)
            for k in range(n):
                d, a, _ = TAPS[t + k]
                acc[d, s - d * a] += y[:, k * 128 : (k + 1) * 128]
            t += n

    for s in range(8):
        apply(s, 0, 3 - min(3, 7 - s), 7 + min(3, s))
        for ci, c in enumerate((-1, 1)):
            for d in (1, 2, 3):
                base = 10 + ci * 9 + (d - 1) * 3
                apply(s, c * d, base + (0 if s + d <= 7 else 1), base + (3 if s - d >= 0 else 2))

    for g in range(8):
        for b in range(4):
            rows = jnp.dot(st_ref[...], acc[b, g].astype(BF), preferred_element_type=F32).astype(BF)
            for j in range(8):
                out_ref[g * 8 + j, :, b * 128 : (b + 1) * 128] = rows[j * ROWS : (j + 1) * ROWS]


def _final_kernel(in_ref, proj_ref, cls_ref, lab_ref, u_ref, v_ref, out_ref, loss_ref, pyr):
    for h in range(2):
        for xq in range(4):
            r = h * 4 + xq
            for zl in range(2):
                total = in_ref[((h * 4 + 0) * 2 + zl) * 4 + xq].astype(F32)
                for y in range(1, 4):
                    total = total + in_ref[((h * 4 + y) * 2 + zl) * 4 + xq].astype(F32)
                total = jnp.maximum(total, 0.0).astype(BF)
                for b in range(4):
                    pyr[r * ROWS : (r + 1) * ROWS, b * 256 + zl * 128 : b * 256 + (zl + 1) * 128] = total[
                        :, b * 128 : (b + 1) * 128
                    ]
    mixed = jnp.dot(pyr[...], proj_ref[...], preferred_element_type=F32)
    projected = jnp.maximum(mixed, 0.0).astype(BF)
    out_ref[...] = jnp.dot(u_ref[...], projected, preferred_element_type=F32).astype(BF)
    rows = jnp.dot(v_ref[...], projected, preferred_element_type=F32).astype(BF)
    logits = lax.dot_general(cls_ref[...], rows, (((1,), (1,)), ((), ())), preferred_element_type=F32)
    total = jnp.zeros((1, 216), F32)
    chosen = jnp.zeros((1, 216), F32)
    for k in range(3):
        total = total + jnp.exp(logits[k : k + 1])
        chosen = chosen + jnp.where(lab_ref[...] == k, logits[k : k + 1], 0.0)
    loss_ref[...] = jnp.log(total) - chosen


def body(features, atrous_weight, point_weight, branch_shift, proj_weight, class_weight, labels):
    x, zh = lax.axis_index("x"), lax.axis_index("zh")
    core, y = lax.axis_index("core"), lax.axis_index("y")
    where = jnp.stack([x, core, zh, y]).astype(jnp.int32)

    wide = atrous_weight.transpose(0, 1, 2, 4, 3)
    taps = [
        point_weight.T if d == 0 else wide[d - 1, a + 1, c + 1]
        for d, a, c in TAPS
    ]
    high = branch_shift.reshape(1, 128).astype(BF)
    rest = branch_shift.reshape(1, 128) - high.astype(F32)
    middle = rest.astype(BF)
    low = (rest - middle.astype(F32)).astype(BF)
    extra = jnp.concatenate([high, middle, low, jnp.zeros((29, 128), BF)])
    weights = jnp.stack(taps + [extra])
    swapped = lax.ppermute(weights, "zh", [(0, 1), (1, 0)])
    pair = jnp.stack([weights, swapped])

    flat = features.transpose(1, 2, 0, 3).reshape(216, 2048)
    messages = pl.pallas_call(
        _pack_kernel,
        out_shape=jax.ShapeDtypeStruct((64, ROWS, 512), BF),
        compiler_params=pltpu.CompilerParams(vmem_limit_bytes=32 * MIB),
        name="pack",
    )(jnp.asarray(_pack_matrix(), BF), flat)

    gathered = [pair] + [
        lax.ppermute(pair, "x", [(i, (i - k) % 4) for i in range(4)]) for k in (1, 2, 3)
    ]
    raw = lax.all_to_all(messages, ("zh", "y", "zl", "x"), 0, 0, tiled=True)
    own = jnp.stack(gathered)
    other = lax.ppermute(own, "core", [(0, 1), (1, 0)])

    shift = _shift_matrices()
    partial = pl.pallas_call(
        _conv_kernel,
        out_shape=jax.ShapeDtypeStruct((64, ROWS, 512), BF),
        in_specs=[
            pl.BlockSpec(memory_space=pltpu.SMEM),
            pl.BlockSpec(memory_space=pltpu.VMEM),
            pl.BlockSpec(memory_space=pltpu.VMEM),
            pl.BlockSpec(memory_space=pltpu.VMEM),
            pl.BlockSpec(memory_space=pl.ANY),
            pl.BlockSpec(memory_space=pl.ANY),
        ],
        scratch_shapes=[
            pltpu.VMEM((7, 8, GRID, 512), BF),
            pltpu.VMEM((28, 4, 32, 512), BF),
            pltpu.VMEM((4, 32, 128), BF),
            pltpu.VMEM((4, 8, GRID, 128), F32),
            pltpu.SemaphoreType.DMA((20,)),
        ],
        compiler_params=pltpu.CompilerParams(vmem_limit_bytes=48 * MIB),
        name="conv",
    )(where, raw, jnp.asarray(shift, BF), jnp.asarray(shift[3].T, BF), own, other)

    arrived = lax.all_to_all(partial, ("zh", "y", "zl", "x"), 0, 0, tiled=True)
    by_cols, by_samples = _unpack_matrices()
    classes = jnp.concatenate([class_weight.T, jnp.zeros((5, 256), BF)])
    projected, loss = pl.pallas_call(
        _final_kernel,
        out_shape=(jax.ShapeDtypeStruct((216, 256), BF), jax.ShapeDtypeStruct((1, 216), F32)),
        scratch_shapes=[pltpu.VMEM((256, 1024), BF)],
        compiler_params=pltpu.CompilerParams(vmem_limit_bytes=32 * MIB),
        name="final",
    )(
        arrived,
        proj_weight,
        classes,
        labels.transpose(1, 0, 2).reshape(1, 216),
        jnp.asarray(by_cols, BF),
        jnp.asarray(by_samples, BF),
    )
    return (
        projected.reshape(6, 18, 2, 256).transpose(2, 0, 1, 3),
        loss.reshape(6, 2, 18).transpose(1, 0, 2),
    )


def solution(mesh):
    fine = Mesh(mesh.devices.reshape(2, 4, 2, 2, 4), ("zh", "y", "core", "zl", "x"))
    tile, chan = ("zh", "y", "core"), ("zl", "x")
    return jax.shard_map(
        body,
        mesh=fine,
        in_specs=(
            P(None, tile, chan, None),
            P(None, None, None, tile, chan),
            P(tile, chan),
            P(None, chan),
            P(),
            P(),
            P(None, tile, chan),
        ),
        out_specs=(P(None, tile, chan, None), P(None, tile, chan)),
        check_vma=False,
    )
```

```python
import jax
import jax.numpy as jnp
import numpy as np
from jax import lax
from jax.experimental import pallas as pl
from jax.experimental.pallas import tpu as pltpu
from jax.sharding import Mesh, PartitionSpec as P

SPOTS = 27
ROWS = 112
GRID = 224
HALO = 18
BF = jnp.bfloat16
F32 = jnp.float32
MIB = 1024 * 1024
JOIN_FLOPS = 4000000000


def _spot(i, t, c):
    return i * 9 + t * 3 + c


def _pack_matrix():
    m = np.zeros((256, 216), np.float32)
    for xq in range(4):
        for h in range(2):
            for i in range(3):
                for t in range(3):
                    for c in range(3):
                        row = (xq % 2) * 3 + i
                        col = 3 * (2 * t + h) + c
                        m[(xq * 2 + h) * 32 + _spot(i, t, c), (row * 18 + col) * 2 + xq // 2] = 1
    return m


def _unpack_matrices():
    by_cols = np.zeros((216, 256), np.float32)
    by_samples = np.zeros((216, 256), np.float32)
    for h in range(2):
        for xq in range(4):
            for i in range(3):
                for t in range(3):
                    for c in range(3):
                        row = (xq % 2) * 3 + i
                        col = 3 * (2 * t + h) + c
                        b = xq // 2
                        src = (h * 4 + xq) * 32 + _spot(i, t, c)
                        by_cols[(row * 18 + col) * 2 + b, src] = 1
                        by_samples[(row * 2 + b) * 18 + col, src] = 1
    return by_cols, by_samples


GROUPS = [
    [(0, 0, 0), (1, 0, 0), (2, 0, 0), (3, 0, 0)],
    [(3, -1, 0), (2, -1, 0), (1, -1, 0), (1, 1, 0), (2, 1, 0), (3, 1, 0)],
] + [[(d, a, c) for a in (-1, 0, 1)] for d in (1, 2, 3) for c in (-1, 1)]
TAPS = [tap for group in GROUPS for tap in group]


def _weights_kernel(wide_ref, point_ref, shift_ref, out_ref, terms):
    for n, (d, a, c) in enumerate(TAPS):
        out_ref[n] = point_ref[...] if d == 0 else wide_ref[(d - 1) * 9 + (a + 1) * 3 + c + 1]
    whole = shift_ref[...]
    high = whole.astype(BF).astype(F32)
    middle = (whole - high).astype(BF).astype(F32)
    terms[...] = jnp.zeros_like(terms)
    terms[0:4, 0:32] = high
    terms[8:12, 0:32] = middle
    terms[16:20, 0:32] = whole - high - middle
    out_ref[28] = terms[...].astype(BF)


def _join_kernel(a_ref, b_ref, c_ref, out_ref):
    for n, ref in enumerate((a_ref, b_ref, c_ref)):
        out_ref[n] = ref[...]


def _pack_kernel(p_ref, f_ref, out_ref, lines):
    p = p_ref[...]
    lines[...] = jnp.zeros_like(lines)
    for y in range(4):
        for z in range(2):
            part = f_ref[:, z * 1024 + y * 256 : z * 1024 + (y + 1) * 256]
            rows = jnp.dot(p, part, preferred_element_type=F32)
            for n in range(8):
                for o in range(2):
                    start = (z * 2 + o) * SPOTS
                    lines[y * 8 + n, start : start + SPOTS] = rows[n * 32 : n * 32 + SPOTS, o * 128 : (o + 1) * 128]
        for n in range(8):
            message = lines[y * 8 + n].astype(BF)
            for zl in range(2):
                out_ref[(((n % 2) * 4 + y) * 2 + zl) * 4 + n // 2] = message


def _conv_kernel(where_ref, raw_ref, near_own, far_own, near_other, far_other, out_ref, lines, grid, xs, wt, sh, acc, outs, sems):
    x, core, zh, first = where_ref[0], where_ref[1], where_ref[2], where_ref[3]
    copies = []
    own_refs = (near_own.at[0], near_own.at[1], far_own, near_own.at[2])
    other_refs = (near_other.at[0], near_other.at[1], far_other, near_other.at[2])
    for k in range(4):
        xo = lax.rem(x + k, 4)
        for z in range(2):
            for o, ref in enumerate((own_refs[k], other_refs[k])):
                slab = lax.rem(zh + z, 2) * 2 + lax.rem(core + o, 2)
                copies.append(
                    pltpu.make_async_copy(
                        ref.at[z, pl.ds(0, 28)],
                        wt.at[:, xo, :, pl.ds(pl.multiple_of(slab * 128, 128), 128)],
                        sems.at[len(copies)],
                    )
                )
        copies.append(pltpu.make_async_copy(own_refs[k].at[0, 28], sh.at[xo], sems.at[len(copies)]))
    for copy in copies:
        copy.start()

    grid[...] = jnp.zeros_like(grid)
    outs[...] = jnp.zeros_like(outs)

    def gather(s):
        for j in range(8):
            lines[s % 2, j] = raw_ref[s * 8 + j].astype(F32)
            for q in range(4):
                for i in range(3):
                    start = q * SPOTS + i * 9
                    grid[s % 2, q, i, HALO + j * 9 : HALO + j * 9 + 9] = lines[s % 2, j, start : start + 9]
        for dc in range(-3, 4):
            for q in range(4):
                rows = [grid[s % 2, q, i, HALO + dc * 6 : HALO + dc * 6 + 72] for i in range(3)]
                rows.append(jnp.zeros((GRID - 216, 128), F32))
                xs[s % 2, dc + 3, :, q * 128 : (q + 1) * 128] = jnp.concatenate(rows, axis=0).astype(BF)

    def multiply(s):
        base = 0
        for n, group in enumerate(GROUPS):
            valid = [t for t, (d, a, _) in enumerate(group) if 0 <= s - d * a < 8]
            for t in range(valid[0], valid[-1] + 1, 2):
                taps = group[t : min(t + 2, valid[-1] + 1)]
                w = wt[base + t : base + t + len(taps)].reshape(len(taps) * 128, 512)
                y = lax.dot_general(
                    xs[s % 2, taps[0][0] * taps[0][2] + 3], w, (((1,), (1,)), ((), ())), preferred_element_type=F32
                )
                for k, (d, a, _) in enumerate(taps):
                    part = y[:, k * 128 : (k + 1) * 128]
                    g = s - d * a
                    if (d, g) in reached:
                        acc[d, g] += part
                    else:
                        acc[d, g] = part
                        reached.add((d, g))
            base += len(group)

    def send(g):
        for j in range(8):
            for b in range(4):
                for i in range(3):
                    start = b * SPOTS + i * 9
                    outs[j, start : start + 9] = acc[b, g, i * 72 + j * 9 : i * 72 + j * 9 + 9] + shifts[b]
            out_ref[g * 8 + j] = outs[j].astype(BF)

    reached = set()
    gather(0)
    for copy in copies:
        copy.wait()

    lane = lax.broadcasted_iota(jnp.int32, (1, 128), 1)
    shifts = []
    for b in range(4):
        line = jnp.zeros((1, 128), F32)
        for xo in range(4):
            terms = sh[xo].astype(F32)
            whole = (terms[0:8] + terms[8:16] + terms[16:24])[b : b + 1]
            if xo > 0:
                whole = pltpu.roll(whole, xo * 32, 1)
            line = jnp.where((lane >= xo * 32) & (lane < xo * 32 + 32), whole, line)
        shifts.append(jnp.where(first == 0, line, 0.0))

    for s in range(8):
        if s < 7:
            gather(s + 1)
        multiply(s)
        if s >= 3:
            send(s - 3)
    for g in range(5, 8):
        send(g)


CONV_SCRATCH = [
    pltpu.VMEM((2, 8, ROWS, 128), F32),
    pltpu.VMEM((2, 4, 3, HALO + 72 + HALO + 4, 128), F32),
    pltpu.VMEM((2, 7, GRID, 512), BF),
    pltpu.VMEM((28, 4, 32, 512), BF),
    pltpu.VMEM((4, 32, 128), BF),
    pltpu.VMEM((4, 8, GRID, 128), F32),
    pltpu.VMEM((8, ROWS, 128), F32),
    pltpu.SemaphoreType.DMA((20,)),
]


def _final_kernel(in_ref, proj_ref, cls_ref, lab_ref, u_ref, v_ref, out_ref, loss_ref, lines, pyr):
    lines[...] = jnp.zeros_like(lines)
    for h in range(2):
        for xq in range(4):
            r = h * 4 + xq
            for zl in range(2):
                total = in_ref[((h * 4 + 0) * 2 + zl) * 4 + xq].astype(F32)
                for y in range(1, 4):
                    total = total + in_ref[((h * 4 + y) * 2 + zl) * 4 + xq].astype(F32)
                lines[r * 2 + zl, 0:ROWS] = jnp.maximum(total, 0.0)
                for b in range(4):
                    pyr[r * 32 : (r + 1) * 32, b * 256 + zl * 128 : b * 256 + (zl + 1) * 128] = lines[
                        r * 2 + zl, b * SPOTS : b * SPOTS + 32
                    ].astype(BF)
    mixed = jnp.dot(pyr[...], proj_ref[...], preferred_element_type=F32)
    projected = jnp.maximum(mixed, 0.0).astype(BF)
    out_ref[...] = jnp.dot(u_ref[...], projected, preferred_element_type=F32).astype(BF)
    rows = jnp.dot(v_ref[...], projected, preferred_element_type=F32).astype(BF)
    logits = lax.dot_general(cls_ref[...], rows, (((1,), (1,)), ((), ())), preferred_element_type=F32)
    total = jnp.zeros((1, 216), F32)
    chosen = jnp.zeros((1, 216), F32)
    for k in range(3):
        total = total + jnp.exp(logits[k : k + 1])
        chosen = chosen + jnp.where(lab_ref[...] == k, logits[k : k + 1], 0.0)
    loss = jnp.log(total) - chosen
    for r in range(12):
        line = loss if r == 0 else pltpu.roll(loss, 216 - r * 18, 1)
        loss_ref[r // 2, r % 2 : r % 2 + 1, :] = line[:, :18]


def body(features, atrous_weight, point_weight, branch_shift, proj_weight, class_weight, labels):
    x, zh = lax.axis_index("x"), lax.axis_index("zh")
    core, y = lax.axis_index("core"), lax.axis_index("y")
    where = jnp.stack([x, core, zh, y]).astype(jnp.int32)

    weights = pl.pallas_call(
        _weights_kernel,
        out_shape=jax.ShapeDtypeStruct((29, 32, 128), BF),
        scratch_shapes=[pltpu.VMEM((32, 128), F32)],
        name="weights",
    )(atrous_weight.transpose(0, 1, 2, 4, 3).reshape(27, 32, 128), point_weight.T, branch_shift)
    swapped = lax.ppermute(weights, "zh", [(0, 1), (1, 0)])

    flat = features.transpose(1, 2, 0, 3).reshape(216, 2048)
    messages = pl.pallas_call(
        _pack_kernel,
        out_shape=jax.ShapeDtypeStruct((64, ROWS, 128), BF),
        scratch_shapes=[pltpu.VMEM((32, ROWS, 128), F32)],
        compiler_params=pltpu.CompilerParams(vmem_limit_bytes=32 * MIB),
        name="pack",
    )(jnp.asarray(_pack_matrix(), BF), flat)

    messages, swapped = lax.optimization_barrier((messages, swapped))
    pair = jnp.stack([weights, swapped])
    def step(piece, k):
        return lax.ppermute(piece, "x", [(i, (i - k) % 4) for i in range(4)])

    def swap(piece):
        return lax.ppermute(piece, "core", [(0, 1), (1, 0)])

    right, left = step(pair, 1), step(pair, -1)
    near_own = pl.pallas_call(
        _join_kernel,
        out_shape=jax.ShapeDtypeStruct((3, 2, 29, 32, 128), BF),
        cost_estimate=pl.CostEstimate(flops=JOIN_FLOPS, bytes_accessed=2800000, transcendentals=0),
        name="join",
    )(pair, right, left)
    far_own = jnp.stack([step(right[0], 1), step(left[1], -1)])
    near_other, far_other = swap(near_own), swap(far_own)
    raw = lax.all_to_all(messages, ("zh", "y", "zl", "x"), 0, 0, tiled=True)
    partial = pl.pallas_call(
        _conv_kernel,
        out_shape=jax.ShapeDtypeStruct((64, ROWS, 128), BF),
        in_specs=[
            pl.BlockSpec(memory_space=pltpu.SMEM),
            pl.BlockSpec(memory_space=pltpu.VMEM),
        ]
        + [pl.BlockSpec(memory_space=pl.ANY)] * 4,
        scratch_shapes=CONV_SCRATCH,
        compiler_params=pltpu.CompilerParams(vmem_limit_bytes=40 * MIB),
        name="conv",
    )(where, raw, near_own, far_own, near_other, far_other)

    arrived = lax.all_to_all(partial, ("zh", "y", "zl", "x"), 0, 0, tiled=True)
    by_cols, by_samples = _unpack_matrices()
    classes = jnp.concatenate([class_weight.T, jnp.zeros((5, 256), BF)])
    projected, loss = pl.pallas_call(
        _final_kernel,
        out_shape=(jax.ShapeDtypeStruct((216, 256), BF), jax.ShapeDtypeStruct((6, 2, 18), F32)),
        scratch_shapes=[pltpu.VMEM((16, ROWS + 8, 128), F32), pltpu.VMEM((256, 1024), BF)],
        compiler_params=pltpu.CompilerParams(vmem_limit_bytes=32 * MIB),
        name="final",
    )(
        arrived,
        proj_weight,
        classes,
        labels.transpose(1, 0, 2).reshape(1, 216),
        jnp.asarray(by_cols, BF),
        jnp.asarray(by_samples, BF),
    )
    return (
        projected.reshape(6, 18, 2, 256).transpose(2, 0, 1, 3),
        loss.transpose(1, 0, 2),
    )


def solution(mesh):
    fine = Mesh(mesh.devices.reshape(2, 4, 2, 2, 4), ("zh", "y", "core", "zl", "x"))
    tile, chan = ("zh", "y", "core"), ("zl", "x")
    return jax.shard_map(
        body,
        mesh=fine,
        in_specs=(
            P(None, tile, chan, None),
            P(None, None, None, tile, chan),
            P(tile, chan),
            P(None, chan),
            P(),
            P(),
            P(None, tile, chan),
        ),
        out_specs=(P(None, tile, chan, None), P(None, tile, chan)),
        check_vma=False,
    )
```

```python
import jax
import jax.numpy as jnp
import numpy as np
from jax import lax
from jax.experimental import pallas as pl
from jax.experimental.pallas import tpu as pltpu
from jax.sharding import Mesh, PartitionSpec as P

SPOTS = 27
ROWS = 112
GRID = 224
HALO = 18
BF = jnp.bfloat16
F32 = jnp.float32
MIB = 1024 * 1024
PICK_FLOPS = 20000000000


def _spot(i, t, c):
    return i * 9 + t * 3 + c


def _pack_matrix():
    m = np.zeros((256, 216), np.float32)
    for xq in range(4):
        for h in range(2):
            for i in range(3):
                for t in range(3):
                    for c in range(3):
                        row = (xq % 2) * 3 + i
                        col = 3 * (2 * t + h) + c
                        m[(xq * 2 + h) * 32 + _spot(i, t, c), (row * 18 + col) * 2 + xq // 2] = 1
    return m


def _unpack_matrices():
    by_cols = np.zeros((216, 256), np.float32)
    by_samples = np.zeros((216, 256), np.float32)
    for h in range(2):
        for xq in range(4):
            for i in range(3):
                for t in range(3):
                    for c in range(3):
                        row = (xq % 2) * 3 + i
                        col = 3 * (2 * t + h) + c
                        b = xq // 2
                        src = (h * 4 + xq) * 32 + _spot(i, t, c)
                        by_cols[(row * 18 + col) * 2 + b, src] = 1
                        by_samples[(row * 2 + b) * 18 + col, src] = 1
    return by_cols, by_samples


GROUPS = [
    [(0, 0, 0), (1, 0, 0), (2, 0, 0), (3, 0, 0)],
    [(3, -1, 0), (2, -1, 0), (1, -1, 0), (1, 1, 0), (2, 1, 0), (3, 1, 0)],
] + [[(d, a, c) for a in (-1, 0, 1)] for d in (1, 2, 3) for c in (-1, 1)]
TAPS = [tap for group in GROUPS for tap in group]


def _weights_kernel(wide_ref, point_ref, shift_ref, out_ref, terms):
    for n, (d, a, c) in enumerate(TAPS):
        out_ref[n] = point_ref[...] if d == 0 else wide_ref[(d - 1) * 9 + (a + 1) * 3 + c + 1]
    whole = shift_ref[...]
    high = whole.astype(BF).astype(F32)
    middle = (whole - high).astype(BF).astype(F32)
    terms[...] = jnp.zeros_like(terms)
    terms[0:4, 0:32] = high
    terms[8:12, 0:32] = middle
    terms[16:20, 0:32] = whole - high - middle
    out_ref[28] = terms[...].astype(BF)


def _pick_kernel(core_ref, a_ref, b_ref, out_ref):
    @pl.when(core_ref[0] == 0)
    def _():
        out_ref[...] = a_ref[...]

    @pl.when(core_ref[0] == 1)
    def _():
        out_ref[...] = b_ref[...]


def _pack_kernel(p_ref, f_ref, out_ref, lines):
    p = p_ref[...]
    lines[...] = jnp.zeros_like(lines)
    for q in range(4):
        rows = jnp.dot(p, f_ref[:, q * 512 : (q + 1) * 512], preferred_element_type=F32)
        for n in range(8):
            for o in range(4):
                lines[q * 8 + n, o * SPOTS : (o + 1) * SPOTS] = rows[n * 32 : n * 32 + SPOTS, o * 128 : (o + 1) * 128]
            message = lines[q * 8 + n].astype(BF)
            for zl in range(2):
                out_ref[((q * 2 + n % 2) * 2 + zl) * 4 + n // 2] = message


def _conv_kernel(where_ref, raw_ref, *refs):
    own_refs, other_refs, out_ref = refs[:4], refs[4:8], refs[8]
    lines, grid, xs, wt, sh, acc, outs, sems = refs[9:]
    x, core, half, first = where_ref[0], where_ref[1], where_ref[2], where_ref[3]
    copies = []
    for k in range(4):
        xo = lax.rem(x + k, 4)
        for z in range(2):
            for o, ref in enumerate((own_refs[k], other_refs[k])):
                slab = lax.rem(half + z, 2) * 2 + lax.rem(core + o, 2)
                copies.append(
                    pltpu.make_async_copy(
                        ref.at[z, pl.ds(0, 28)],
                        wt.at[:, xo, :, pl.ds(pl.multiple_of(slab * 128, 128), 128)],
                        sems.at[len(copies)],
                    )
                )
        copies.append(pltpu.make_async_copy(own_refs[k].at[0, 28], sh.at[xo], sems.at[len(copies)]))
    for copy in copies:
        copy.start()

    grid[...] = jnp.zeros_like(grid)
    outs[...] = jnp.zeros_like(outs)

    def gather(s):
        for j in range(8):
            lines[s % 2, j] = raw_ref[s * 8 + j].astype(F32)
            for q in range(4):
                for i in range(3):
                    start = q * SPOTS + i * 9
                    grid[s % 2, q, i, HALO + j * 9 : HALO + j * 9 + 9] = lines[s % 2, j, start : start + 9]
        for dc in range(-3, 4):
            for q in range(4):
                rows = [grid[s % 2, q, i, HALO + dc * 6 : HALO + dc * 6 + 72] for i in range(3)]
                rows.append(jnp.zeros((GRID - 216, 128), F32))
                xs[s % 2, dc + 3, :, q * 128 : (q + 1) * 128] = jnp.concatenate(rows, axis=0).astype(BF)

    def multiply(s):
        base = 0
        for n, group in enumerate(GROUPS):
            valid = [t for t, (d, a, _) in enumerate(group) if 0 <= s - d * a < 8]
            for t in range(valid[0], valid[-1] + 1, 2):
                taps = group[t : min(t + 2, valid[-1] + 1)]
                w = wt[base + t : base + t + len(taps)].reshape(len(taps) * 128, 512)
                y = lax.dot_general(
                    xs[s % 2, taps[0][0] * taps[0][2] + 3], w, (((1,), (1,)), ((), ())), preferred_element_type=F32
                )
                for k, (d, a, _) in enumerate(taps):
                    part = y[:, k * 128 : (k + 1) * 128]
                    g = s - d * a
                    if (d, g) in reached:
                        acc[d, g] += part
                    else:
                        acc[d, g] = part
                        reached.add((d, g))
            base += len(group)

    def send(g):
        for j in range(8):
            for b in range(4):
                for i in range(3):
                    start = b * SPOTS + i * 9
                    outs[j, start : start + 9] = acc[b, g, i * 72 + j * 9 : i * 72 + j * 9 + 9] + shifts[b]
            out_ref[g * 8 + j] = outs[j].astype(BF)

    reached = set()
    gather(0)
    for copy in copies:
        copy.wait()

    lane = lax.broadcasted_iota(jnp.int32, (1, 128), 1)
    shifts = []
    for b in range(4):
        line = jnp.zeros((1, 128), F32)
        for xo in range(4):
            terms = sh[xo].astype(F32)
            whole = (terms[0:8] + terms[8:16] + terms[16:24])[b : b + 1]
            if xo > 0:
                whole = pltpu.roll(whole, xo * 32, 1)
            line = jnp.where((lane >= xo * 32) & (lane < xo * 32 + 32), whole, line)
        shifts.append(jnp.where(first == 0, line, 0.0))

    for s in range(8):
        if s < 7:
            gather(s + 1)
        multiply(s)
        if s >= 3:
            send(s - 3)
    for g in range(5, 8):
        send(g)


CONV_SCRATCH = [
    pltpu.VMEM((2, 8, ROWS, 128), F32),
    pltpu.VMEM((2, 4, 3, HALO + 72 + HALO + 4, 128), F32),
    pltpu.VMEM((2, 7, GRID, 512), BF),
    pltpu.VMEM((28, 4, 32, 512), BF),
    pltpu.VMEM((4, 32, 128), BF),
    pltpu.VMEM((4, 8, GRID, 128), F32),
    pltpu.VMEM((8, ROWS, 128), F32),
    pltpu.SemaphoreType.DMA((20,)),
]


def _final_kernel(in_ref, proj_ref, cls_ref, lab_ref, u_ref, v_ref, out_ref, loss_ref, lines, pyr):
    lines[...] = jnp.zeros_like(lines)
    for h in range(2):
        for xq in range(4):
            r = h * 4 + xq
            for zl in range(2):
                total = in_ref[(h * 2 + zl) * 4 + xq].astype(F32)
                for q in range(1, 4):
                    total = total + in_ref[((q * 2 + h) * 2 + zl) * 4 + xq].astype(F32)
                lines[r * 2 + zl, 0:ROWS] = jnp.maximum(total, 0.0)
                for b in range(4):
                    pyr[r * 32 : (r + 1) * 32, b * 256 + zl * 128 : b * 256 + (zl + 1) * 128] = lines[
                        r * 2 + zl, b * SPOTS : b * SPOTS + 32
                    ].astype(BF)
    mixed = jnp.dot(pyr[...], proj_ref[...], preferred_element_type=F32)
    projected = jnp.maximum(mixed, 0.0).astype(BF)
    out_ref[...] = jnp.dot(u_ref[...], projected, preferred_element_type=F32).astype(BF)
    rows = jnp.dot(v_ref[...], projected, preferred_element_type=F32).astype(BF)
    logits = lax.dot_general(cls_ref[...], rows, (((1,), (1,)), ((), ())), preferred_element_type=F32)
    total = jnp.zeros((1, 216), F32)
    chosen = jnp.zeros((1, 216), F32)
    for k in range(3):
        total = total + jnp.exp(logits[k : k + 1])
        chosen = chosen + jnp.where(lab_ref[...] == k, logits[k : k + 1], 0.0)
    loss = jnp.log(total) - chosen
    for r in range(12):
        line = loss if r == 0 else pltpu.roll(loss, 216 - r * 18, 1)
        loss_ref[r // 2, r % 2 : r % 2 + 1, :] = line[:, :18]


def body(features, atrous_weight, point_weight, branch_shift, proj_weight, class_weight, labels):
    x, zh = lax.axis_index("x"), lax.axis_index("zh")
    core, y = lax.axis_index("core"), lax.axis_index("y")
    where = jnp.stack([x, core, y % 2, zh * 2 + y // 2]).astype(jnp.int32)

    weights = pl.pallas_call(
        _weights_kernel,
        out_shape=jax.ShapeDtypeStruct((29, 32, 128), BF),
        scratch_shapes=[pltpu.VMEM((32, 128), F32)],
        name="weights",
    )(atrous_weight.transpose(0, 1, 2, 4, 3).reshape(27, 32, 128), point_weight.T, branch_shift)
    swapped = lax.ppermute(weights, "y", [(0, 1), (1, 0), (2, 3), (3, 2)])

    flat = features.transpose(1, 2, 0, 3).reshape(216, 2048)
    messages = pl.pallas_call(
        _pack_kernel,
        out_shape=jax.ShapeDtypeStruct((64, ROWS, 128), BF),
        scratch_shapes=[pltpu.VMEM((32, ROWS, 128), F32)],
        compiler_params=pltpu.CompilerParams(vmem_limit_bytes=32 * MIB),
        name="pack",
    )(jnp.asarray(_pack_matrix(), BF), flat)

    messages, swapped = lax.optimization_barrier((messages, swapped))
    pair = jnp.stack([weights, swapped])
    def swap(piece):
        return lax.ppermute(piece, "core", [(0, 1), (1, 0)])

    right = lax.ppermute(pair, "x", [(i, (i - 1) % 4) for i in range(4)])
    left = lax.ppermute(pair, "x", [(i, (i + 1) % 4) for i in range(4)])
    picked = pl.pallas_call(
        _pick_kernel,
        out_shape=jax.ShapeDtypeStruct(pair.shape, BF),
        in_specs=[
            pl.BlockSpec(memory_space=pltpu.SMEM),
            pl.BlockSpec(memory_space=pltpu.VMEM),
            pl.BlockSpec(memory_space=pltpu.VMEM),
        ],
        cost_estimate=pl.CostEstimate(flops=PICK_FLOPS, bytes_accessed=1400000, transcendentals=0),
        name="pick",
    )(core.astype(jnp.int32).reshape(1), right, left)
    far = lax.ppermute(
        picked, ("core", "x"), [(c * 4 + i, c * 4 + (i - 1 + 2 * c) % 4) for c in range(2) for i in range(4)]
    )
    own = [pair, right, far, left]
    other = [swap(piece) for piece in own]
    raw = lax.all_to_all(messages, ("zh", "y", "zl", "x"), 0, 0, tiled=True)
    partial = pl.pallas_call(
        _conv_kernel,
        out_shape=jax.ShapeDtypeStruct((64, ROWS, 128), BF),
        in_specs=[pl.BlockSpec(memory_space=pltpu.SMEM), pl.BlockSpec(memory_space=pltpu.VMEM)]
        + [pl.BlockSpec(memory_space=pl.ANY)] * 8,
        out_specs=pl.BlockSpec(memory_space=pltpu.VMEM),
        scratch_shapes=CONV_SCRATCH,
        compiler_params=pltpu.CompilerParams(vmem_limit_bytes=24 * MIB),
        name="conv",
    )(where, raw, *own, *other)

    arrived = lax.all_to_all(partial, ("zh", "y", "zl", "x"), 0, 0, tiled=True)
    by_cols, by_samples = _unpack_matrices()
    classes = jnp.concatenate([class_weight.T, jnp.zeros((5, 256), BF)])
    projected, loss = pl.pallas_call(
        _final_kernel,
        out_shape=(jax.ShapeDtypeStruct((216, 256), BF), jax.ShapeDtypeStruct((6, 2, 18), F32)),
        scratch_shapes=[pltpu.VMEM((16, ROWS + 8, 128), F32), pltpu.VMEM((256, 1024), BF)],
        compiler_params=pltpu.CompilerParams(vmem_limit_bytes=32 * MIB),
        name="final",
    )(
        arrived,
        proj_weight,
        classes,
        labels.transpose(1, 0, 2).reshape(1, 216),
        jnp.asarray(by_cols, BF),
        jnp.asarray(by_samples, BF),
    )
    return (
        projected.reshape(6, 18, 2, 256).transpose(2, 0, 1, 3),
        loss.transpose(1, 0, 2),
    )


def solution(mesh):
    fine = Mesh(mesh.devices.reshape(2, 4, 2, 2, 4), ("zh", "y", "core", "zl", "x"))
    tile, chan = ("zh", "y", "core"), ("zl", "x")
    return jax.shard_map(
        body,
        mesh=fine,
        in_specs=(
            P(None, tile, chan, None),
            P(None, None, None, tile, chan),
            P(tile, chan),
            P(None, chan),
            P(),
            P(),
            P(None, tile, chan),
        ),
        out_specs=(P(None, tile, chan, None), P(None, tile, chan)),
        check_vma=False,
    )
```

```python
import itertools

import jax
import jax.numpy as jnp
import numpy as np
from jax import lax
from jax.experimental import pallas as pl
from jax.experimental.pallas import tpu as pltpu
from jax.sharding import Mesh, PartitionSpec as P

SPOTS = 27
ROWS = 112
GRID = 224
HALO = 18
BF = jnp.bfloat16
F32 = jnp.float32
MIB = 1024 * 1024
PICK_FLOPS = 20000000000


def _spot(i, t, c):
    return i * 9 + t * 3 + c


def _pack_matrix():
    m = np.zeros((256, 216), np.float32)
    for xq in range(4):
        for h in range(2):
            for i in range(3):
                for t in range(3):
                    for c in range(3):
                        row = (xq % 2) * 3 + i
                        col = 3 * (2 * t + h) + c
                        m[(xq * 2 + h) * 32 + _spot(i, t, c), (row * 18 + col) * 2 + xq // 2] = 1
    return m


def _unpack_matrices():
    by_cols = np.zeros((2, 108, 256), np.float32)
    by_samples = np.zeros((216, 256), np.float32)
    for h in range(2):
        for xq in range(4):
            for i in range(3):
                for t in range(3):
                    for c in range(3):
                        row = (xq % 2) * 3 + i
                        col = 3 * (2 * t + h) + c
                        b = xq // 2
                        src = (h * 4 + xq) * 32 + _spot(i, t, c)
                        by_cols[b, row * 18 + col, src] = 1
                        by_samples[(row * 2 + b) * 18 + col, src] = 1
    return by_cols, by_samples


GROUPS = [
    [(0, 0, 0), (1, 0, 0), (2, 0, 0), (3, 0, 0)],
    [(3, -1, 0), (2, -1, 0), (1, -1, 0), (1, 1, 0), (2, 1, 0), (3, 1, 0)],
] + [[(d, a, c) for a in (-1, 0, 1)] for d in (1, 2, 3) for c in (-1, 1)]
TAPS = [tap for group in GROUPS for tap in group]


def _weights_kernel(wide_ref, point_ref, shift_ref, out_ref, terms):
    for n, (d, a, c) in enumerate(TAPS):
        out_ref[n] = point_ref[...] if d == 0 else wide_ref[(d - 1) * 9 + (a + 1) * 3 + c + 1]
    whole = shift_ref[...]
    high = whole.astype(BF).astype(F32)
    middle = (whole - high).astype(BF).astype(F32)
    terms[...] = jnp.zeros_like(terms)
    terms[0:4, 0:32] = high
    terms[8:12, 0:32] = middle
    terms[16:20, 0:32] = whole - high - middle
    out_ref[28] = terms[...].astype(BF)


def _pick_kernel(core_ref, a_ref, b_ref, out_ref):
    @pl.when(core_ref[0] == 0)
    def _():
        out_ref[...] = a_ref[...]

    @pl.when(core_ref[0] == 1)
    def _():
        out_ref[...] = b_ref[...]


def _pack_kernel(p_ref, f_ref, out_ref, lines):
    p = p_ref[...]
    lines[...] = jnp.zeros_like(lines)
    for q in range(4):
        rows = jnp.dot(p, f_ref[:, q * 512 : (q + 1) * 512], preferred_element_type=F32)
        for n in range(8):
            for o in range(4):
                lines[q * 8 + n, o * SPOTS : (o + 1) * SPOTS] = rows[n * 32 : n * 32 + SPOTS, o * 128 : (o + 1) * 128]
            message = lines[q * 8 + n].astype(BF)
            for zl in range(2):
                out_ref[((q * 2 + n % 2) * 2 + zl) * 4 + n // 2] = message


def _conv_kernel(where_ref, raw_ref, *refs):
    own_refs, other_refs, out_ref = refs[:4], refs[4:8], refs[8]
    lines, grid, xs, wt, sh, acc, outs, sems = refs[9:]
    x, core, half, first = where_ref[0], where_ref[1], where_ref[2], where_ref[3]
    copies = []
    for k in range(4):
        xo = lax.rem(x + k, 4)
        for z in range(2):
            for o, ref in enumerate((own_refs[k], other_refs[k])):
                slab = lax.rem(half + z, 2) * 2 + lax.rem(core + o, 2)
                copies.append(
                    pltpu.make_async_copy(
                        ref.at[z, pl.ds(0, 28)],
                        wt.at[:, xo, :, pl.ds(pl.multiple_of(slab * 128, 128), 128)],
                        sems.at[len(copies)],
                    )
                )
        copies.append(pltpu.make_async_copy(own_refs[k].at[0, 28], sh.at[xo], sems.at[len(copies)]))
    for copy in copies:
        copy.start()

    grid[...] = jnp.zeros_like(grid)
    outs[...] = jnp.zeros_like(outs)

    def window(dc):
        low = max(0, -dc * 6) // 8 * 8
        high = -(-min(72, 72 - dc * 6) // 8) * 8
        return low, high - low, -(-3 * (high - low) // 16) * 16

    def gather(s):
        for j in range(8):
            lines[s % 2, j] = raw_ref[s * 8 + j].astype(F32)
            for q in range(4):
                for i in range(3):
                    start = q * SPOTS + i * 9
                    grid[s % 2, q, i, HALO + j * 9 : HALO + j * 9 + 9] = lines[s % 2, j, start : start + 9]
            yield
        for dc in range(-3, 4):
            for q in range(4):
                low, size, full = window(dc)
                start = HALO + dc * 6 + low
                rows = [grid[s % 2, q, i, start : start + size] for i in range(3)]
                if full > 3 * size:
                    rows.append(jnp.zeros((full - 3 * size, 128), F32))
                rows = jnp.concatenate(rows, axis=0).astype(BF)
                xs[s // 2 % 2, dc + 3, s % 2 * full : (s % 2 + 1) * full, q * 128 : (q + 1) * 128] = rows
                yield

    def multiply(m):
        base = 0
        for group in GROUPS:
            valid = [t for t, (d, a, _) in enumerate(group) if _meets(m, d, a)]
            for t in range(valid[0], valid[-1] + 1, 2):
                taps = group[t : min(t + 2, valid[-1] + 1)]
                w = wt[base + t : base + t + len(taps)].reshape(len(taps) * 128, 512)
                dc = taps[0][0] * taps[0][2]
                low, size, full = window(dc)
                y = lax.dot_general(
                    xs[m % 2, dc + 3, : 2 * full], w, (((1,), (1,)), ((), ())), preferred_element_type=F32
                )
                for k, (d, a, _) in enumerate(taps):
                    for n in range(2):
                        g = 2 * m + n - d * a
                        if not 0 <= g < 8:
                            continue
                        part = y[n * full : (n + 1) * full, k * 128 : (k + 1) * 128]
                        if (d, g) not in reached:
                            acc[d, g] = part
                            reached.add((d, g))
                        elif size == 72:
                            acc[d, g] += part
                        else:
                            for i in range(3):
                                acc[d, g, i * 72 + low : i * 72 + low + size] += part[i * size : (i + 1) * size]
                yield
            base += len(group)

    def send(g):
        for j in range(8):
            for b in range(4):
                for i in range(3):
                    start = b * SPOTS + i * 9
                    outs[j, start : start + 9] = acc[b, g, i * 72 + j * 9 : i * 72 + j * 9 + 9] + shifts[b]
            out_ref[g * 8 + j] = outs[j].astype(BF)
            yield

    reached = set()
    for _ in itertools.chain(gather(0), gather(1)):
        pass
    for copy in copies:
        copy.wait()

    lane = lax.broadcasted_iota(jnp.int32, (1, 128), 1)
    shifts = []
    for b in range(4):
        line = jnp.zeros((1, 128), F32)
        for xo in range(4):
            terms = sh[xo].astype(F32)
            whole = (terms[0:8] + terms[8:16] + terms[16:24])[b : b + 1]
            if xo > 0:
                whole = pltpu.roll(whole, xo * 32, 1)
            line = jnp.where((lane >= xo * 32) & (lane < xo * 32 + 32), whole, line)
        shifts.append(jnp.where(first == 0, line, 0.0))

    for m in range(4):
        beside = []
        if m == 3:
            beside.extend((send(g), 8) for g in range(3))
        else:
            beside.extend((gather(s), 36) for s in (2 * m + 2, 2 * m + 3))
        left = sum(n for _, n in beside)
        steps = itertools.chain(*(step for step, _ in beside))
        tiles = _tiles(m)
        for n, _ in enumerate(multiply(m)):
            share = -(-left // max(tiles - n, 1))
            for _ in range(share):
                next(steps, None)
            left -= share
        for _ in steps:
            pass
    for g in range(3, 8):
        for _ in send(g):
            pass


def _meets(m, d, a):
    return any(0 <= s - d * a < 8 for s in (2 * m, 2 * m + 1))


def _tiles(m):
    return sum(-(-sum(_meets(m, d, a) for d, a, _ in group) // 2) for group in GROUPS)


CONV_SCRATCH = [
    pltpu.VMEM((2, 8, ROWS, 128), F32),
    pltpu.VMEM((2, 4, 3, HALO + 72 + HALO + 4, 128), F32),
    pltpu.VMEM((2, 7, 2 * GRID, 512), BF),
    pltpu.VMEM((28, 4, 32, 512), BF),
    pltpu.VMEM((4, 32, 128), BF),
    pltpu.VMEM((4, 8, GRID, 128), F32),
    pltpu.VMEM((8, ROWS, 128), F32),
    pltpu.SemaphoreType.DMA((20,)),
]


def _final_kernel(in_ref, proj_ref, cls_ref, lab_ref, u_ref, v_ref, out_ref, loss_ref, lines, pyr):
    lines[...] = jnp.zeros_like(lines)
    for h in range(2):
        for xq in range(4):
            r = h * 4 + xq
            for zl in range(2):
                total = in_ref[(h * 2 + zl) * 4 + xq].astype(F32)
                for q in range(1, 4):
                    total = total + in_ref[((q * 2 + h) * 2 + zl) * 4 + xq].astype(F32)
                lines[r * 2 + zl, 0:ROWS] = jnp.maximum(total, 0.0)
                for b in range(4):
                    pyr[r * 32 : (r + 1) * 32, b * 256 + zl * 128 : b * 256 + (zl + 1) * 128] = lines[
                        r * 2 + zl, b * SPOTS : b * SPOTS + 32
                    ].astype(BF)
    mixed = jnp.dot(pyr[...], proj_ref[...], preferred_element_type=F32)
    projected = jnp.maximum(mixed, 0.0).astype(BF)
    for b in range(2):
        out_ref[:, b, :] = jnp.dot(u_ref[b], projected, preferred_element_type=F32).astype(BF)
    rows = jnp.dot(v_ref[...], projected, preferred_element_type=F32).astype(BF)
    logits = lax.dot_general(cls_ref[...], rows, (((1,), (1,)), ((), ())), preferred_element_type=F32)
    total = jnp.zeros((1, 216), F32)
    chosen = jnp.zeros((1, 216), F32)
    for k in range(3):
        total = total + jnp.exp(logits[k : k + 1])
        chosen = chosen + jnp.where(lab_ref[...] == k, logits[k : k + 1], 0.0)
    loss = jnp.log(total) - chosen
    for r in range(12):
        line = loss if r == 0 else pltpu.roll(loss, 216 - r * 18, 1)
        loss_ref[r // 2, r % 2 : r % 2 + 1, :] = line[:, :18]


def body(features, atrous_weight, point_weight, branch_shift, proj_weight, class_weight, labels):
    x, zh = lax.axis_index("x"), lax.axis_index("zh")
    core, y = lax.axis_index("core"), lax.axis_index("y")
    where = jnp.stack([x, core, y % 2, zh * 2 + y // 2]).astype(jnp.int32)

    weights = pl.pallas_call(
        _weights_kernel,
        out_shape=jax.ShapeDtypeStruct((29, 32, 128), BF),
        scratch_shapes=[pltpu.VMEM((32, 128), F32)],
        name="weights",
    )(atrous_weight.transpose(0, 1, 2, 4, 3).reshape(27, 32, 128), point_weight.T, branch_shift)
    swapped = lax.ppermute(weights, "y", [(0, 1), (1, 0), (2, 3), (3, 2)])

    flat = features.transpose(1, 2, 0, 3).reshape(216, 2048)
    messages = pl.pallas_call(
        _pack_kernel,
        out_shape=jax.ShapeDtypeStruct((64, ROWS, 128), BF),
        scratch_shapes=[pltpu.VMEM((32, ROWS, 128), F32)],
        compiler_params=pltpu.CompilerParams(vmem_limit_bytes=32 * MIB),
        name="pack",
    )(jnp.asarray(_pack_matrix(), BF), flat)

    messages, swapped = lax.optimization_barrier((messages, swapped))
    pair = jnp.stack([weights, swapped])
    def swap(piece):
        return lax.ppermute(piece, "core", [(0, 1), (1, 0)])

    right = lax.ppermute(pair, "x", [(i, (i - 1) % 4) for i in range(4)])
    left = lax.ppermute(pair, "x", [(i, (i + 1) % 4) for i in range(4)])
    picked = pl.pallas_call(
        _pick_kernel,
        out_shape=jax.ShapeDtypeStruct(pair.shape, BF),
        in_specs=[pl.BlockSpec(memory_space=pltpu.SMEM)] + [pl.BlockSpec(memory_space=pltpu.VMEM)] * 2,
        cost_estimate=pl.CostEstimate(flops=PICK_FLOPS, bytes_accessed=1400000, transcendentals=0),
        name="pick",
    )(core.astype(jnp.int32).reshape(1), right, left)
    far = lax.ppermute(
        picked, ("core", "x"), [(c * 4 + i, c * 4 + (i - 1 + 2 * c) % 4) for c in range(2) for i in range(4)]
    )
    own = [pair, right, far, left]
    other = [swap(piece) for piece in own]
    raw = lax.all_to_all(messages, ("zh", "y", "zl", "x"), 0, 0, tiled=True)
    partial = pl.pallas_call(
        _conv_kernel,
        out_shape=jax.ShapeDtypeStruct((64, ROWS, 128), BF),
        in_specs=[pl.BlockSpec(memory_space=pltpu.SMEM), pl.BlockSpec(memory_space=pltpu.VMEM)]
        + [pl.BlockSpec(memory_space=pl.ANY)] * 8,
        out_specs=pl.BlockSpec(memory_space=pltpu.VMEM),
        scratch_shapes=CONV_SCRATCH,
        compiler_params=pltpu.CompilerParams(vmem_limit_bytes=24 * MIB),
        name="conv",
    )(where, raw, *own, *other)

    arrived = lax.all_to_all(partial, ("zh", "y", "zl", "x"), 0, 0, tiled=True)
    by_cols, by_samples = _unpack_matrices()
    classes = jnp.concatenate([class_weight.T, jnp.zeros((5, 256), BF)])
    projected, loss = pl.pallas_call(
        _final_kernel,
        out_shape=(jax.ShapeDtypeStruct((108, 2, 256), BF), jax.ShapeDtypeStruct((6, 2, 18), F32)),
        scratch_shapes=[pltpu.VMEM((16, ROWS + 8, 128), F32), pltpu.VMEM((256, 1024), BF)],
        compiler_params=pltpu.CompilerParams(vmem_limit_bytes=32 * MIB),
        name="final",
    )(
        arrived,
        proj_weight,
        classes,
        labels.transpose(1, 0, 2).reshape(1, 216),
        jnp.asarray(by_cols, BF),
        jnp.asarray(by_samples, BF),
    )
    return (
        projected.reshape(6, 18, 2, 256).transpose(2, 0, 1, 3),
        loss.transpose(1, 0, 2),
    )


def solution(mesh):
    fine = Mesh(mesh.devices.reshape(2, 4, 2, 2, 4), ("zh", "y", "core", "zl", "x"))
    tile, chan = ("zh", "y", "core"), ("zl", "x")
    return jax.shard_map(
        body,
        mesh=fine,
        in_specs=(
            P(None, tile, chan, None),
            P(None, None, None, tile, chan),
            P(tile, chan),
            P(None, chan),
            P(),
            P(),
            P(None, tile, chan),
        ),
        out_specs=(P(None, tile, chan, None), P(None, tile, chan)),
        check_vma=False,
    )
```

```python
import itertools

import jax
import jax.numpy as jnp
import numpy as np
from jax import lax
from jax.experimental import pallas as pl
from jax.experimental.pallas import tpu as pltpu
from jax.sharding import Mesh, PartitionSpec as P

SPOTS = 27
ROWS = 112
GRID = 224
HALO = 18
BF = jnp.bfloat16
F32 = jnp.float32
MIB = 1024 * 1024
PICK_FLOPS = 20000000000


def _spot(i, t, c):
    return i * 9 + t * 3 + c


def _pack_matrix():
    m = np.zeros((256, 216), np.float32)
    for xq in range(4):
        for h in range(2):
            for i in range(3):
                for t in range(3):
                    for c in range(3):
                        row = (xq % 2) * 3 + i
                        col = 3 * (2 * t + h) + c
                        m[(xq * 2 + h) * 32 + _spot(i, t, c), (row * 18 + col) * 2 + xq // 2] = 1
    return m


def _unpack_matrices():
    by_cols = np.zeros((2, 108, 256), np.float32)
    by_samples = np.zeros((216, 256), np.float32)
    for h in range(2):
        for xq in range(4):
            for i in range(3):
                for t in range(3):
                    for c in range(3):
                        row = (xq % 2) * 3 + i
                        col = 3 * (2 * t + h) + c
                        b = xq // 2
                        src = (h * 4 + xq) * 32 + _spot(i, t, c)
                        by_cols[b, row * 18 + col, src] = 1
                        by_samples[(row * 2 + b) * 18 + col, src] = 1
    return by_cols, by_samples


GROUPS = [
    [(0, 0, 0), (1, 0, 0), (2, 0, 0), (3, 0, 0)],
    [(3, -1, 0), (2, -1, 0), (1, -1, 0), (1, 1, 0), (2, 1, 0), (3, 1, 0)],
] + [[(d, a, c) for a in (-1, 0, 1)] for d in (1, 2, 3) for c in (-1, 1)]
TAPS = [tap for group in GROUPS for tap in group]


def _weights_kernel(wide_ref, point_ref, shift_ref, out_ref, terms):
    for n, (d, a, c) in enumerate(TAPS):
        out_ref[n] = point_ref[...] if d == 0 else wide_ref[(d - 1) * 9 + (a + 1) * 3 + c + 1]
    whole = shift_ref[...]
    high = whole.astype(BF).astype(F32)
    middle = (whole - high).astype(BF).astype(F32)
    terms[...] = jnp.zeros_like(terms)
    terms[0:4, 0:32] = high
    terms[8:12, 0:32] = middle
    terms[16:20, 0:32] = whole - high - middle
    out_ref[28] = terms[...].astype(BF)


def _pick_kernel(core_ref, a_ref, b_ref, out_ref):
    @pl.when(core_ref[0] == 0)
    def _():
        out_ref[...] = a_ref[...]

    @pl.when(core_ref[0] == 1)
    def _():
        out_ref[...] = b_ref[...]


def _pack_kernel(p_ref, f_ref, out_ref, lines):
    p = p_ref[...]
    lines[...] = jnp.zeros_like(lines)
    for q in range(4):
        rows = jnp.dot(p, f_ref[:, q * 512 : (q + 1) * 512], preferred_element_type=F32)
        for n in range(8):
            for o in range(4):
                lines[q * 8 + n, o * SPOTS : (o + 1) * SPOTS] = rows[n * 32 : n * 32 + SPOTS, o * 128 : (o + 1) * 128]
            message = lines[q * 8 + n].astype(BF)
            for zl in range(2):
                out_ref[((q * 2 + n % 2) * 2 + zl) * 4 + n // 2] = message


def _conv_kernel(where_ref, raw_ref, *refs):
    own_refs, other_refs, out_ref = refs[:3], refs[3:6], refs[6]
    lines, grid, xs, wt, sh, acc, outs, sems = refs[7:]
    x, core, half, first = where_ref[0], where_ref[1], where_ref[2], where_ref[3]
    own_refs, other_refs = (
        (near, sides.at[0], far, sides.at[1]) for near, sides, far in (own_refs, other_refs)
    )
    copies = []
    for k in range(4):
        xo = lax.rem(x + k, 4)
        for z in range(2):
            for o, ref in enumerate((own_refs[k], other_refs[k])):
                slab = lax.rem(half + z, 2) * 2 + lax.rem(core + o, 2)
                copies.append(
                    pltpu.make_async_copy(
                        ref.at[z, pl.ds(0, 28)],
                        wt.at[:, xo, :, pl.ds(pl.multiple_of(slab * 128, 128), 128)],
                        sems.at[len(copies)],
                    )
                )
        copies.append(pltpu.make_async_copy(own_refs[k].at[0, 28], sh.at[xo], sems.at[len(copies)]))
    for copy in copies:
        copy.start()

    grid[...] = jnp.zeros_like(grid)
    outs[...] = jnp.zeros_like(outs)

    def window(dc):
        low = max(0, -dc * 6) // 8 * 8
        high = -(-min(72, 72 - dc * 6) // 8) * 8
        return low, high - low, -(-3 * (high - low) // 16) * 16

    def gather(s):
        for j in range(8):
            lines[s % 2, j] = raw_ref[s * 8 + j].astype(F32)
            for q in range(4):
                for i in range(3):
                    start = q * SPOTS + i * 9
                    grid[s % 2, q, i, HALO + j * 9 : HALO + j * 9 + 9] = lines[s % 2, j, start : start + 9]
            yield
        for dc in range(-3, 4):
            for q in range(4):
                low, size, full = window(dc)
                start = HALO + dc * 6 + low
                rows = [grid[s % 2, q, i, start : start + size] for i in range(3)]
                if full > 3 * size:
                    rows.append(jnp.zeros((full - 3 * size, 128), F32))
                rows = jnp.concatenate(rows, axis=0).astype(BF)
                xs[s // 2 % 2, dc + 3, s % 2 * full : (s % 2 + 1) * full, q * 128 : (q + 1) * 128] = rows
                yield

    def multiply(m):
        base = 0
        for group in GROUPS:
            valid = [t for t, (d, a, _) in enumerate(group) if _meets(m, d, a)]
            for t in range(valid[0], valid[-1] + 1, 2):
                taps = group[t : min(t + 2, valid[-1] + 1)]
                w = wt[base + t : base + t + len(taps)].reshape(len(taps) * 128, 512)
                dc = taps[0][0] * taps[0][2]
                low, size, full = window(dc)
                y = lax.dot_general(
                    xs[m % 2, dc + 3, : 2 * full], w, (((1,), (1,)), ((), ())), preferred_element_type=F32
                )
                for k, (d, a, _) in enumerate(taps):
                    for n in range(2):
                        g = 2 * m + n - d * a
                        if not 0 <= g < 8:
                            continue
                        part = y[n * full : (n + 1) * full, k * 128 : (k + 1) * 128]
                        if (d, g) not in reached:
                            acc[d, g] = part
                            reached.add((d, g))
                        elif size == 72:
                            acc[d, g] += part
                        else:
                            for i in range(3):
                                acc[d, g, i * 72 + low : i * 72 + low + size] += part[i * size : (i + 1) * size]
                yield
            base += len(group)

    def send(g):
        for j in range(8):
            for b in range(4):
                for i in range(3):
                    start = b * SPOTS + i * 9
                    outs[j, start : start + 9] = acc[b, g, i * 72 + j * 9 : i * 72 + j * 9 + 9] + shifts[b]
            out_ref[g * 8 + j] = outs[j].astype(BF)
            yield

    reached = set()
    for _ in itertools.chain(gather(0), gather(1)):
        pass
    for copy in copies:
        copy.wait()

    lane = lax.broadcasted_iota(jnp.int32, (1, 128), 1)
    shifts = []
    for b in range(4):
        line = jnp.zeros((1, 128), F32)
        for xo in range(4):
            terms = sh[xo].astype(F32)
            whole = (terms[0:8] + terms[8:16] + terms[16:24])[b : b + 1]
            if xo > 0:
                whole = pltpu.roll(whole, xo * 32, 1)
            line = jnp.where((lane >= xo * 32) & (lane < xo * 32 + 32), whole, line)
        shifts.append(jnp.where(first == 0, line, 0.0))

    for m in range(4):
        beside = []
        if m == 3:
            beside.extend((send(g), 8) for g in range(3))
        else:
            beside.extend((gather(s), 36) for s in (2 * m + 2, 2 * m + 3))
        left = sum(n for _, n in beside)
        steps = itertools.chain(*(step for step, _ in beside))
        tiles = _tiles(m)
        for n, _ in enumerate(multiply(m)):
            share = -(-left // max(tiles - n, 1))
            for _ in range(share):
                next(steps, None)
            left -= share
        for _ in steps:
            pass
    for g in range(3, 8):
        for _ in send(g):
            pass


def _meets(m, d, a):
    return any(0 <= s - d * a < 8 for s in (2 * m, 2 * m + 1))


def _tiles(m):
    return sum(-(-sum(_meets(m, d, a) for d, a, _ in group) // 2) for group in GROUPS)


CONV_SCRATCH = [
    pltpu.VMEM((2, 8, ROWS, 128), F32),
    pltpu.VMEM((2, 4, 3, HALO + 72 + HALO + 4, 128), F32),
    pltpu.VMEM((2, 7, 2 * GRID, 512), BF),
    pltpu.VMEM((28, 4, 32, 512), BF),
    pltpu.VMEM((4, 32, 128), BF),
    pltpu.VMEM((4, 8, GRID, 128), F32),
    pltpu.VMEM((8, ROWS, 128), F32),
    pltpu.SemaphoreType.DMA((20,)),
]


def _final_kernel(in_ref, proj_ref, cls_ref, lab_ref, u_ref, v_ref, out_ref, loss_ref, lines, pyr):
    lines[...] = jnp.zeros_like(lines)
    for h in range(2):
        for xq in range(4):
            r = h * 4 + xq
            for zl in range(2):
                total = in_ref[(h * 2 + zl) * 4 + xq].astype(F32)
                for q in range(1, 4):
                    total = total + in_ref[((q * 2 + h) * 2 + zl) * 4 + xq].astype(F32)
                lines[r * 2 + zl, 0:ROWS] = jnp.maximum(total, 0.0)
                for b in range(4):
                    pyr[r * 32 : (r + 1) * 32, b * 256 + zl * 128 : b * 256 + (zl + 1) * 128] = lines[
                        r * 2 + zl, b * SPOTS : b * SPOTS + 32
                    ].astype(BF)
    mixed = jnp.dot(pyr[...], proj_ref[...], preferred_element_type=F32)
    projected = jnp.maximum(mixed, 0.0).astype(BF)
    for b in range(2):
        out_ref[:, b, :] = jnp.dot(u_ref[b], projected, preferred_element_type=F32).astype(BF)
    rows = jnp.dot(v_ref[...], projected, preferred_element_type=F32).astype(BF)
    logits = lax.dot_general(cls_ref[...], rows, (((1,), (1,)), ((), ())), preferred_element_type=F32)
    total = jnp.zeros((1, 216), F32)
    chosen = jnp.zeros((1, 216), F32)
    for k in range(3):
        total = total + jnp.exp(logits[k : k + 1])
        chosen = chosen + jnp.where(lab_ref[...] == k, logits[k : k + 1], 0.0)
    loss = jnp.log(total) - chosen
    for r in range(12):
        line = loss if r == 0 else pltpu.roll(loss, 216 - r * 18, 1)
        loss_ref[r // 2, r % 2 : r % 2 + 1, :] = line[:, :18]


def body(features, atrous_weight, point_weight, branch_shift, proj_weight, class_weight, labels):
    x, zh = lax.axis_index("x"), lax.axis_index("zh")
    core, y = lax.axis_index("core"), lax.axis_index("y")
    where = jnp.stack([x, core, y % 2, zh * 2 + y // 2]).astype(jnp.int32)

    weights = pl.pallas_call(
        _weights_kernel,
        out_shape=jax.ShapeDtypeStruct((29, 32, 128), BF),
        scratch_shapes=[pltpu.VMEM((32, 128), F32)],
        name="weights",
    )(atrous_weight.transpose(0, 1, 2, 4, 3).reshape(27, 32, 128), point_weight.T, branch_shift)
    swapped = lax.ppermute(weights, "y", [(0, 1), (1, 0), (2, 3), (3, 2)])

    flat = features.transpose(1, 2, 0, 3).reshape(216, 2048)
    messages = pl.pallas_call(
        _pack_kernel,
        out_shape=jax.ShapeDtypeStruct((64, ROWS, 128), BF),
        scratch_shapes=[pltpu.VMEM((32, ROWS, 128), F32)],
        compiler_params=pltpu.CompilerParams(vmem_limit_bytes=32 * MIB),
        name="pack",
    )(jnp.asarray(_pack_matrix(), BF), flat)

    messages, swapped = lax.optimization_barrier((messages, swapped))
    pair = jnp.stack([weights, swapped])
    def swap(piece):
        return lax.ppermute(piece, "core", [(0, 1), (1, 0)])

    right = lax.ppermute(pair, "x", [(i, (i - 1) % 4) for i in range(4)])
    left = lax.ppermute(pair, "x", [(i, (i + 1) % 4) for i in range(4)])
    picked = pl.pallas_call(
        _pick_kernel,
        out_shape=jax.ShapeDtypeStruct(pair.shape, BF),
        in_specs=[pl.BlockSpec(memory_space=pltpu.SMEM)] + [pl.BlockSpec(memory_space=pltpu.VMEM)] * 2,
        cost_estimate=pl.CostEstimate(flops=PICK_FLOPS, bytes_accessed=1400000, transcendentals=0),
        name="pick",
    )(core.astype(jnp.int32).reshape(1), right, left)
    far = lax.ppermute(
        picked, ("core", "x"), [(c * 4 + i, c * 4 + (i - 1 + 2 * c) % 4) for c in range(2) for i in range(4)]
    )
    sides = jnp.stack([right, left])
    own = [pair, sides, far]
    other = [swap(piece) for piece in own]
    raw = lax.all_to_all(messages, ("zh", "y", "zl", "x"), 0, 0, tiled=True)
    partial = pl.pallas_call(
        _conv_kernel,
        out_shape=jax.ShapeDtypeStruct((64, ROWS, 128), BF),
        in_specs=[pl.BlockSpec(memory_space=pltpu.SMEM), pl.BlockSpec(memory_space=pltpu.VMEM)]
        + [pl.BlockSpec(memory_space=pl.ANY)] * 6,
        out_specs=pl.BlockSpec(memory_space=pltpu.VMEM),
        scratch_shapes=CONV_SCRATCH,
        compiler_params=pltpu.CompilerParams(vmem_limit_bytes=24 * MIB),
        name="conv",
    )(where, raw, *own, *other)

    arrived = lax.all_to_all(partial, ("zh", "y", "zl", "x"), 0, 0, tiled=True)
    by_cols, by_samples = _unpack_matrices()
    classes = jnp.concatenate([class_weight.T, jnp.zeros((5, 256), BF)])
    projected, loss = pl.pallas_call(
        _final_kernel,
        out_shape=(jax.ShapeDtypeStruct((108, 2, 256), BF), jax.ShapeDtypeStruct((6, 2, 18), F32)),
        scratch_shapes=[pltpu.VMEM((16, ROWS + 8, 128), F32), pltpu.VMEM((256, 1024), BF)],
        compiler_params=pltpu.CompilerParams(vmem_limit_bytes=32 * MIB),
        name="final",
    )(
        arrived,
        proj_weight,
        classes,
        labels.transpose(1, 0, 2).reshape(1, 216),
        jnp.asarray(by_cols, BF),
        jnp.asarray(by_samples, BF),
    )
    return (
        projected.reshape(6, 18, 2, 256).transpose(2, 0, 1, 3),
        loss.transpose(1, 0, 2),
    )


def solution(mesh):
    fine = Mesh(mesh.devices.reshape(2, 4, 2, 2, 4), ("zh", "y", "core", "zl", "x"))
    tile, chan = ("zh", "y", "core"), ("zl", "x")
    return jax.shard_map(
        body,
        mesh=fine,
        in_specs=(
            P(None, tile, chan, None),
            P(None, None, None, tile, chan),
            P(tile, chan),
            P(None, chan),
            P(),
            P(),
            P(None, tile, chan),
        ),
        out_specs=(P(None, tile, chan, None), P(None, tile, chan)),
        check_vma=False,
    )
```

```python
import itertools

import jax
import jax.numpy as jnp
import numpy as np
from jax import lax
from jax.experimental import pallas as pl
from jax.experimental.pallas import tpu as pltpu
from jax.sharding import Mesh, PartitionSpec as P

SPOTS = 27
ROWS = 112
GRID = 224
HALO = 18
BF = jnp.bfloat16
F32 = jnp.float32
MIB = 1024 * 1024
PICK_FLOPS = 20000000000


def _spot(i, t, c):
    return i * 9 + t * 3 + c


def _pack_matrix():
    m = np.zeros((256, 216), np.float32)
    for xq in range(4):
        for h in range(2):
            for i in range(3):
                for t in range(3):
                    for c in range(3):
                        row = (xq % 2) * 3 + i
                        col = 3 * (2 * t + h) + c
                        m[(xq * 2 + h) * 32 + _spot(i, t, c), (row * 18 + col) * 2 + xq // 2] = 1
    return m


def _unpack_matrices():
    by_cols = np.zeros((2, 108, 256), np.float32)
    by_samples = np.zeros((216, 256), np.float32)
    for h in range(2):
        for xq in range(4):
            for i in range(3):
                for t in range(3):
                    for c in range(3):
                        row = (xq % 2) * 3 + i
                        col = 3 * (2 * t + h) + c
                        b = xq // 2
                        src = (h * 4 + xq) * 32 + _spot(i, t, c)
                        by_cols[b, row * 18 + col, src] = 1
                        by_samples[(row * 2 + b) * 18 + col, src] = 1
    return by_cols, by_samples


GROUPS = [
    [(0, 0, 0), (1, 0, 0), (2, 0, 0), (3, 0, 0)],
    [(3, -1, 0), (2, -1, 0), (1, -1, 0), (1, 1, 0), (2, 1, 0), (3, 1, 0)],
] + [[(d, a, c) for a in (-1, 0, 1)] for d in (1, 2, 3) for c in (-1, 1)]
TAPS = [tap for group in GROUPS for tap in group]


def _weights_kernel(wide_ref, point_ref, out_ref):
    for n, (d, a, c) in enumerate(TAPS):
        out_ref[n] = point_ref[...] if d == 0 else wide_ref[(d - 1) * 9 + (a + 1) * 3 + c + 1]


def _pick_kernel(core_ref, a_ref, b_ref, out_ref):
    @pl.when(core_ref[0] == 0)
    def _():
        out_ref[...] = a_ref[...]

    @pl.when(core_ref[0] == 1)
    def _():
        out_ref[...] = b_ref[...]


def _pack_kernel(p_ref, f_ref, out_ref, lines):
    p = p_ref[...]
    lines[...] = jnp.zeros_like(lines)
    for q in range(4):
        rows = jnp.dot(p, f_ref[:, q * 512 : (q + 1) * 512], preferred_element_type=F32)
        for n in range(8):
            for o in range(4):
                lines[q * 8 + n, o * SPOTS : (o + 1) * SPOTS] = rows[n * 32 : n * 32 + SPOTS, o * 128 : (o + 1) * 128]
            message = lines[q * 8 + n].astype(BF)
            for zl in range(2):
                out_ref[((q * 2 + n % 2) * 2 + zl) * 4 + n // 2] = message


def _conv_kernel(where_ref, raw_ref, shift_ref, *refs):
    own_refs, other_refs, out_ref = refs[:3], refs[3:6], refs[6]
    lines, grid, xs, wt, acc, outs, sems = refs[7:]
    x, core, half = where_ref[0], where_ref[1], where_ref[2]
    own_refs, other_refs = (
        (near, sides.at[0], far, sides.at[1]) for near, sides, far in (own_refs, other_refs)
    )
    copies = []
    for k in range(4):
        xo = lax.rem(x + k, 4)
        for z in range(2):
            for o, ref in enumerate((own_refs[k], other_refs[k])):
                slab = lax.rem(half + z, 2) * 2 + lax.rem(core + o, 2)
                copies.append(
                    pltpu.make_async_copy(
                        ref.at[z],
                        wt.at[:, xo, :, pl.ds(pl.multiple_of(slab * 128, 128), 128)],
                        sems.at[len(copies)],
                    )
                )
    for copy in copies:
        copy.start()

    grid[...] = jnp.zeros_like(grid)
    outs[...] = jnp.zeros_like(outs)
    whole = shift_ref[...]
    high = whole.astype(BF).astype(F32)
    middle = (whole - high).astype(BF).astype(F32)
    for j in range(8):
        for n, term in enumerate((high, middle, whole - high - middle)):
            outs[j, 4 * SPOTS + n : 4 * SPOTS + n + 1] = term

    def window(dc):
        low = max(0, -dc * 6) // 8 * 8
        high = -(-min(72, 72 - dc * 6) // 8) * 8
        return low, high - low, -(-3 * (high - low) // 16) * 16

    def gather(s):
        for j in range(8):
            lines[s % 2, j] = raw_ref[s * 8 + j].astype(F32)
            for q in range(4):
                for i in range(3):
                    start = q * SPOTS + i * 9
                    grid[s % 2, q, i, HALO + j * 9 : HALO + j * 9 + 9] = lines[s % 2, j, start : start + 9]
            yield
        for dc in range(-3, 4):
            for q in range(4):
                low, size, full = window(dc)
                start = HALO + dc * 6 + low
                rows = [grid[s % 2, q, i, start : start + size] for i in range(3)]
                if full > 3 * size:
                    rows.append(jnp.zeros((full - 3 * size, 128), F32))
                rows = jnp.concatenate(rows, axis=0).astype(BF)
                xs[s // 2 % 2, dc + 3, s % 2 * full : (s % 2 + 1) * full, q * 128 : (q + 1) * 128] = rows
                yield

    def multiply(m):
        base = 0
        for group in GROUPS:
            valid = [t for t, (d, a, _) in enumerate(group) if _meets(m, d, a)]
            for t in range(valid[0], valid[-1] + 1, 2):
                taps = group[t : min(t + 2, valid[-1] + 1)]
                w = wt[base + t : base + t + len(taps)].reshape(len(taps) * 128, 512)
                dc = taps[0][0] * taps[0][2]
                low, size, full = window(dc)
                y = lax.dot_general(
                    xs[m % 2, dc + 3, : 2 * full], w, (((1,), (1,)), ((), ())), preferred_element_type=F32
                )
                for k, (d, a, _) in enumerate(taps):
                    for n in range(2):
                        g = 2 * m + n - d * a
                        if not 0 <= g < 8:
                            continue
                        part = y[n * full : (n + 1) * full, k * 128 : (k + 1) * 128]
                        if (d, g) not in reached:
                            acc[d, g] = part
                            reached.add((d, g))
                        elif size == 72:
                            acc[d, g] += part
                        else:
                            for i in range(3):
                                acc[d, g, i * 72 + low : i * 72 + low + size] += part[i * size : (i + 1) * size]
                yield
            base += len(group)

    def send(g):
        for j in range(8):
            for b in range(4):
                for i in range(3):
                    start = b * SPOTS + i * 9
                    outs[j, start : start + 9] = acc[b, g, i * 72 + j * 9 : i * 72 + j * 9 + 9]
            out_ref[g * 8 + j] = outs[j].astype(BF)
            yield

    reached = set()
    for _ in itertools.chain(gather(0), gather(1)):
        pass
    for copy in copies:
        copy.wait()

    for m in range(4):
        beside = []
        if m == 3:
            beside.extend((send(g), 8) for g in range(3))
        else:
            beside.extend((gather(s), 36) for s in (2 * m + 2, 2 * m + 3))
        left = sum(n for _, n in beside)
        steps = itertools.chain(*(step for step, _ in beside))
        tiles = _tiles(m)
        for n, _ in enumerate(multiply(m)):
            share = -(-left // max(tiles - n, 1))
            for _ in range(share):
                next(steps, None)
            left -= share
        for _ in steps:
            pass
    for g in range(3, 8):
        for _ in send(g):
            pass


def _meets(m, d, a):
    return any(0 <= s - d * a < 8 for s in (2 * m, 2 * m + 1))


def _tiles(m):
    return sum(-(-sum(_meets(m, d, a) for d, a, _ in group) // 2) for group in GROUPS)


CONV_SCRATCH = [
    pltpu.VMEM((2, 8, ROWS, 128), F32),
    pltpu.VMEM((2, 4, 3, HALO + 72 + HALO + 4, 128), F32),
    pltpu.VMEM((2, 7, 2 * GRID, 512), BF),
    pltpu.VMEM((28, 4, 32, 512), BF),
    pltpu.VMEM((4, 8, GRID, 128), F32),
    pltpu.VMEM((8, ROWS, 128), F32),
    pltpu.SemaphoreType.DMA((16,)),
]


def _final_kernel(in_ref, proj_ref, cls_ref, lab_ref, u_ref, v_ref, out_ref, loss_ref, lines, pyr):
    lines[...] = jnp.zeros_like(lines)
    lane = lax.broadcasted_iota(jnp.int32, (1, 128), 1)
    shifts = {}
    for zl in range(2):
        wholes = []
        for xq in range(4):
            terms = in_ref[zl * 4 + xq, 96:112].astype(F32)
            wholes.append(terms[12:13] + terms[13:14] + terms[14:15])
        for b in range(4):
            line = jnp.zeros((1, 128), F32)
            for xq in range(4):
                whole = wholes[xq] if xq == b else pltpu.roll(wholes[xq], (xq - b) % 4 * 32, 1)
                line = jnp.where((lane >= xq * 32) & (lane < xq * 32 + 32), whole, line)
            shifts[zl, b] = line
    for h in range(2):
        for xq in range(4):
            r = h * 4 + xq
            for zl in range(2):
                total = in_ref[(h * 2 + zl) * 4 + xq].astype(F32)
                for q in range(1, 4):
                    total = total + in_ref[((q * 2 + h) * 2 + zl) * 4 + xq].astype(F32)
                lines[r * 2 + zl, 0:ROWS] = total
                for b in range(4):
                    branch = lines[r * 2 + zl, b * SPOTS : b * SPOTS + 32] + shifts[zl, b]
                    start = b * 256 + zl * 128
                    pyr[r * 32 : (r + 1) * 32, start : start + 128] = jnp.maximum(branch, 0.0).astype(BF)
    mixed = jnp.dot(pyr[...], proj_ref[...], preferred_element_type=F32)
    projected = jnp.maximum(mixed, 0.0).astype(BF)
    for b in range(2):
        out_ref[:, b, :] = jnp.dot(u_ref[b], projected, preferred_element_type=F32).astype(BF)
    rows = jnp.dot(v_ref[...], projected, preferred_element_type=F32).astype(BF)
    logits = lax.dot_general(cls_ref[...], rows, (((1,), (1,)), ((), ())), preferred_element_type=F32)
    total = jnp.zeros((1, 216), F32)
    chosen = jnp.zeros((1, 216), F32)
    for k in range(3):
        total = total + jnp.exp(logits[k : k + 1])
        chosen = chosen + jnp.where(lab_ref[...] == k, logits[k : k + 1], 0.0)
    loss = jnp.log(total) - chosen
    for r in range(12):
        line = loss if r == 0 else pltpu.roll(loss, 216 - r * 18, 1)
        loss_ref[r // 2, r % 2 : r % 2 + 1, :] = line[:, :18]


def body(features, atrous_weight, point_weight, branch_shift, proj_weight, class_weight, labels):
    x, core, y = lax.axis_index("x"), lax.axis_index("core"), lax.axis_index("y")
    where = jnp.stack([x, core, y % 2]).astype(jnp.int32)

    weights = pl.pallas_call(
        _weights_kernel,
        out_shape=jax.ShapeDtypeStruct((28, 32, 128), BF),
        name="weights",
    )(atrous_weight.transpose(0, 1, 2, 4, 3).reshape(27, 32, 128), point_weight.T)
    swapped = lax.ppermute(weights, "y", [(0, 1), (1, 0), (2, 3), (3, 2)])

    flat = features.transpose(1, 2, 0, 3).reshape(216, 2048)
    messages = pl.pallas_call(
        _pack_kernel,
        out_shape=jax.ShapeDtypeStruct((64, ROWS, 128), BF),
        scratch_shapes=[pltpu.VMEM((32, ROWS, 128), F32)],
        compiler_params=pltpu.CompilerParams(vmem_limit_bytes=32 * MIB),
        name="pack",
    )(jnp.asarray(_pack_matrix(), BF), flat)

    messages, swapped = lax.optimization_barrier((messages, swapped))
    pair = jnp.stack([weights, swapped])
    def swap(piece):
        return lax.ppermute(piece, "core", [(0, 1), (1, 0)])

    right = lax.ppermute(pair, "x", [(i, (i - 1) % 4) for i in range(4)])
    left = lax.ppermute(pair, "x", [(i, (i + 1) % 4) for i in range(4)])
    picked = pl.pallas_call(
        _pick_kernel,
        out_shape=jax.ShapeDtypeStruct(pair.shape, BF),
        in_specs=[pl.BlockSpec(memory_space=pltpu.SMEM)] + [pl.BlockSpec(memory_space=pltpu.VMEM)] * 2,
        cost_estimate=pl.CostEstimate(flops=PICK_FLOPS, bytes_accessed=1400000, transcendentals=0),
        name="pick",
    )(core.astype(jnp.int32).reshape(1), right, left)
    far = lax.ppermute(
        picked, ("core", "x"), [(c * 4 + i, c * 4 + (i - 1 + 2 * c) % 4) for c in range(2) for i in range(4)]
    )
    sides = jnp.stack([right, left])
    own = [pair, sides, far]
    other = [swap(piece) for piece in own]
    raw = lax.all_to_all(messages, ("zh", "y", "zl", "x"), 0, 0, tiled=True)
    partial = pl.pallas_call(
        _conv_kernel,
        out_shape=jax.ShapeDtypeStruct((64, ROWS, 128), BF),
        in_specs=[pl.BlockSpec(memory_space=pltpu.SMEM)]
        + [pl.BlockSpec(memory_space=pltpu.VMEM)] * 2
        + [pl.BlockSpec(memory_space=pl.ANY)] * 6,
        out_specs=pl.BlockSpec(memory_space=pltpu.VMEM),
        scratch_shapes=CONV_SCRATCH,
        compiler_params=pltpu.CompilerParams(vmem_limit_bytes=24 * MIB),
        name="conv",
    )(where, raw, branch_shift.reshape(1, 128), *own, *other)

    arrived = lax.all_to_all(partial, ("zh", "y", "zl", "x"), 0, 0, tiled=True)
    by_cols, by_samples = _unpack_matrices()
    classes = jnp.concatenate([class_weight.T, jnp.zeros((5, 256), BF)])
    projected, loss = pl.pallas_call(
        _final_kernel,
        out_shape=(jax.ShapeDtypeStruct((108, 2, 256), BF), jax.ShapeDtypeStruct((6, 2, 18), F32)),
        scratch_shapes=[pltpu.VMEM((16, ROWS + 8, 128), F32), pltpu.VMEM((256, 1024), BF)],
        compiler_params=pltpu.CompilerParams(vmem_limit_bytes=32 * MIB),
        name="final",
    )(
        arrived,
        proj_weight,
        classes,
        labels.transpose(1, 0, 2).reshape(1, 216),
        jnp.asarray(by_cols, BF),
        jnp.asarray(by_samples, BF),
    )
    return (
        projected.reshape(6, 18, 2, 256).transpose(2, 0, 1, 3),
        loss.transpose(1, 0, 2),
    )


def solution(mesh):
    fine = Mesh(mesh.devices.reshape(2, 4, 2, 2, 4), ("zh", "y", "core", "zl", "x"))
    tile, chan = ("zh", "y", "core"), ("zl", "x")
    return jax.shard_map(
        body,
        mesh=fine,
        in_specs=(
            P(None, tile, chan, None),
            P(None, None, None, tile, chan),
            P(tile, chan),
            P(None, chan),
            P(),
            P(),
            P(None, tile, chan),
        ),
        out_specs=(P(None, tile, chan, None), P(None, tile, chan)),
        check_vma=False,
    )
```

```python
import itertools

import jax
import jax.numpy as jnp
import numpy as np
from jax import lax
from jax.experimental import pallas as pl
from jax.experimental.pallas import tpu as pltpu
from jax.sharding import Mesh, PartitionSpec as P

SPOTS = 27
ROWS = 112
GRID = 224
HALO = 18
BF = jnp.bfloat16
F32 = jnp.float32
MIB = 1024 * 1024
PICK_FLOPS = 20000000000


def _spot(i, t, c):
    return i * 9 + t * 3 + c


def _pack_matrix():
    m = np.zeros((256, 216), np.float32)
    for xq in range(4):
        for h in range(2):
            for i in range(3):
                for t in range(3):
                    for c in range(3):
                        row = (xq % 2) * 3 + i
                        col = 3 * (2 * t + h) + c
                        m[(xq * 2 + h) * 32 + _spot(i, t, c), (row * 18 + col) * 2 + xq // 2] = 1
    return m


def _unpack_matrices():
    by_cols = np.zeros((2, 108, 256), np.float32)
    by_samples = np.zeros((216, 256), np.float32)
    for h in range(2):
        for xq in range(4):
            for i in range(3):
                for t in range(3):
                    for c in range(3):
                        row = (xq % 2) * 3 + i
                        col = 3 * (2 * t + h) + c
                        b = xq // 2
                        src = (h * 4 + xq) * 32 + _spot(i, t, c)
                        by_cols[b, row * 18 + col, src] = 1
                        by_samples[(row * 2 + b) * 18 + col, src] = 1
    return by_cols, by_samples


GROUPS = [
    [(0, 0, 0), (1, 0, 0), (2, 0, 0), (3, 0, 0)],
    [(3, -1, 0), (2, -1, 0), (1, -1, 0), (1, 1, 0), (2, 1, 0), (3, 1, 0)],
] + [[(d, a, c) for a in (-1, 0, 1)] for d in (1, 2, 3) for c in (-1, 1)]
TAPS = [tap for group in GROUPS for tap in group]


def _weights_kernel(wide_ref, point_ref, out_ref):
    for n, (d, a, c) in enumerate(TAPS):
        out_ref[n] = point_ref[...] if d == 0 else wide_ref[(d - 1) * 9 + (a + 1) * 3 + c + 1]


def _pick_kernel(core_ref, a_ref, b_ref, out_ref):
    @pl.when(core_ref[0] == 0)
    def _():
        out_ref[...] = a_ref[...]

    @pl.when(core_ref[0] == 1)
    def _():
        out_ref[...] = b_ref[...]


def _pack_kernel(p_ref, f_ref, out_ref, lines):
    p = p_ref[...]
    lines[...] = jnp.zeros_like(lines)
    for q in range(4):
        rows = jnp.dot(p, f_ref[:, q * 512 : (q + 1) * 512], preferred_element_type=F32)
        for n in range(8):
            for o in range(4):
                lines[q * 8 + n, o * SPOTS : (o + 1) * SPOTS] = rows[n * 32 : n * 32 + SPOTS, o * 128 : (o + 1) * 128]
            message = lines[q * 8 + n].astype(BF)
            for zl in range(2):
                out_ref[((q * 2 + n % 2) * 2 + zl) * 4 + n // 2] = message


def _conv_kernel(where_ref, raw_ref, shift_ref, *refs):
    own_refs, other_refs, out_ref = refs[:3], refs[3:6], refs[6]
    lines, grid, xs, wt, acc, outs, sems = refs[7:]
    x, core, half = where_ref[0], where_ref[1], where_ref[2]
    own_refs, other_refs = (
        (near, sides.at[0], far, sides.at[1]) for near, sides, far in (own_refs, other_refs)
    )
    copies = []
    for k in range(4):
        xo = lax.rem(x + k, 4)
        for z in range(2):
            for o, ref in enumerate((own_refs[k], other_refs[k])):
                slab = lax.rem(half + z, 2) * 2 + lax.rem(core + o, 2)
                copies.append(
                    pltpu.make_async_copy(
                        ref.at[z],
                        wt.at[:, xo, :, pl.ds(pl.multiple_of(slab * 128, 128), 128)],
                        sems.at[len(copies)],
                    )
                )
    for copy in copies:
        copy.start()

    grid[...] = jnp.zeros_like(grid)
    outs[...] = jnp.zeros_like(outs)
    whole = shift_ref[...]
    high = whole.astype(BF).astype(F32)
    middle = (whole - high).astype(BF).astype(F32)
    for j in range(8):
        for n, term in enumerate((high, middle, whole - high - middle)):
            outs[j, 4 * SPOTS + n : 4 * SPOTS + n + 1] = term

    def window(dc):
        low = max(0, -dc * 6) // 8 * 8
        high = -(-min(72, 72 - dc * 6) // 8) * 8
        return low, high - low, -(-3 * (high - low) // 16) * 16

    def gather(s):
        for j in range(8):
            lines[s % 2, j] = raw_ref[s * 8 + j].astype(F32)
            for q in range(4):
                for i in range(3):
                    start = q * SPOTS + i * 9
                    grid[s % 2, q, i, HALO + j * 9 : HALO + j * 9 + 9] = lines[s % 2, j, start : start + 9]
            yield
        for dc in range(-3, 4):
            for q in range(4):
                low, size, full = window(dc)
                start = HALO + dc * 6 + low
                rows = [grid[s % 2, q, i, start : start + size] for i in range(3)]
                if full > 3 * size:
                    rows.append(jnp.zeros((full - 3 * size, 128), F32))
                rows = jnp.concatenate(rows, axis=0).astype(BF)
                xs[s // 2 % 2, dc + 3, s % 2 * full : (s % 2 + 1) * full, q * 128 : (q + 1) * 128] = rows
                yield

    def multiply(m):
        base = 0
        for group in GROUPS:
            valid = [t for t, (d, a, _) in enumerate(group) if _meets(m, d, a)]
            for t in range(valid[0], valid[-1] + 1, 2):
                taps = group[t : min(t + 2, valid[-1] + 1)]
                w = wt[base + t : base + t + len(taps)].reshape(len(taps) * 128, 512)
                dc = taps[0][0] * taps[0][2]
                low, size, full = window(dc)
                y = lax.dot_general(
                    xs[m % 2, dc + 3, : 2 * full], w, (((1,), (1,)), ((), ())), preferred_element_type=F32
                )
                for k, (d, a, _) in enumerate(taps):
                    for n in range(2):
                        g = 2 * m + n - d * a
                        if not 0 <= g < 8:
                            continue
                        part = y[n * full : (n + 1) * full, k * 128 : (k + 1) * 128]
                        if (d, g) not in reached:
                            acc[d, g] = part
                            reached.add((d, g))
                        elif size == 72:
                            acc[d, g] += part
                        else:
                            for i in range(3):
                                acc[d, g, i * 72 + low : i * 72 + low + size] += part[i * size : (i + 1) * size]
                yield
            base += len(group)

    def send(g):
        for j in range(8):
            for b in range(4):
                for i in range(3):
                    start = b * SPOTS + i * 9
                    outs[j, start : start + 9] = acc[b, g, i * 72 + j * 9 : i * 72 + j * 9 + 9]
            out_ref[g * 8 + j] = outs[j].astype(BF)
            yield

    reached = set()
    for _ in itertools.chain(gather(0), gather(1)):
        pass
    for copy in copies:
        copy.wait()

    for m in range(4):
        beside = []
        if m == 3:
            beside.extend((send(g), 8) for g in range(3))
        else:
            beside.extend((gather(s), 36) for s in (2 * m + 2, 2 * m + 3))
        left = sum(n for _, n in beside)
        steps = itertools.chain(*(step for step, _ in beside))
        tiles = _tiles(m)
        for n, _ in enumerate(multiply(m)):
            share = -(-left // max(tiles - n, 1))
            for _ in range(share):
                next(steps, None)
            left -= share
        for _ in steps:
            pass
    for g in range(3, 8):
        for _ in send(g):
            pass


def _meets(m, d, a):
    return any(0 <= s - d * a < 8 for s in (2 * m, 2 * m + 1))


def _tiles(m):
    return sum(-(-sum(_meets(m, d, a) for d, a, _ in group) // 2) for group in GROUPS)


CONV_SCRATCH = [
    pltpu.VMEM((2, 8, ROWS, 128), F32),
    pltpu.VMEM((2, 4, 3, HALO + 72 + HALO + 4, 128), F32),
    pltpu.VMEM((2, 7, 2 * GRID, 512), BF),
    pltpu.VMEM((28, 4, 32, 512), BF),
    pltpu.VMEM((4, 8, GRID, 128), F32),
    pltpu.VMEM((8, ROWS, 128), F32),
    pltpu.SemaphoreType.DMA((16,)),
]


def _final_kernel(in_ref, proj_ref, cls_ref, lab_ref, u_ref, v_ref, out_ref, loss_ref, lines, pyr):
    lines[:, ROWS:] = jnp.zeros((16, 8, 128), F32)
    lane = lax.broadcasted_iota(jnp.int32, (1, 128), 1)
    shifts = {}
    for zl in range(2):
        wholes = []
        for xq in range(4):
            terms = in_ref[zl * 4 + xq, 96:112].astype(F32)
            wholes.append(terms[12:13] + terms[13:14] + terms[14:15])
        for b in range(4):
            line = jnp.zeros((1, 128), F32)
            for xq in range(4):
                whole = wholes[xq] if xq == b else pltpu.roll(wholes[xq], (xq - b) % 4 * 32, 1)
                line = jnp.where((lane >= xq * 32) & (lane < xq * 32 + 32), whole, line)
            shifts[zl, b] = line
    for h in range(2):
        for xq in range(4):
            r = h * 4 + xq
            for zl in range(2):
                total = in_ref[(h * 2 + zl) * 4 + xq].astype(F32)
                for q in range(1, 4):
                    total = total + in_ref[((q * 2 + h) * 2 + zl) * 4 + xq].astype(F32)
                lines[r * 2 + zl, 0:ROWS] = total
                for b in range(4):
                    branch = lines[r * 2 + zl, b * SPOTS : b * SPOTS + 32] + shifts[zl, b]
                    start = b * 256 + zl * 128
                    pyr[r * 32 : (r + 1) * 32, start : start + 128] = jnp.maximum(branch, 0.0).astype(BF)
    mixed = jnp.dot(pyr[...], proj_ref[...], preferred_element_type=F32)
    projected = jnp.maximum(mixed, 0.0).astype(BF)
    for b in range(2):
        out_ref[:, b, :] = jnp.dot(u_ref[b], projected, preferred_element_type=F32).astype(BF)
    rows = jnp.dot(v_ref[...], projected, preferred_element_type=F32).astype(BF)
    logits = lax.dot_general(cls_ref[...], rows, (((1,), (1,)), ((), ())), preferred_element_type=F32)
    total = jnp.zeros((1, 216), F32)
    chosen = jnp.zeros((1, 216), F32)
    for k in range(3):
        total = total + jnp.exp(logits[k : k + 1])
        chosen = chosen + jnp.where(lab_ref[...] == k, logits[k : k + 1], 0.0)
    loss = jnp.log(total) - chosen
    for r in range(12):
        line = loss if r == 0 else pltpu.roll(loss, 216 - r * 18, 1)
        loss_ref[r // 2, r % 2 : r % 2 + 1, :] = line[:, :18]


def body(features, atrous_weight, point_weight, branch_shift, proj_weight, class_weight, labels):
    x, core, y = lax.axis_index("x"), lax.axis_index("core"), lax.axis_index("y")
    where = jnp.stack([x, core, y % 2]).astype(jnp.int32)

    weights = pl.pallas_call(
        _weights_kernel,
        out_shape=jax.ShapeDtypeStruct((28, 32, 128), BF),
        name="weights",
    )(atrous_weight.transpose(0, 1, 2, 4, 3).reshape(27, 32, 128), point_weight.T)
    swapped = lax.ppermute(weights, "y", [(0, 1), (1, 0), (2, 3), (3, 2)])

    flat = features.transpose(1, 2, 0, 3).reshape(216, 2048)
    messages = pl.pallas_call(
        _pack_kernel,
        out_shape=jax.ShapeDtypeStruct((64, ROWS, 128), BF),
        scratch_shapes=[pltpu.VMEM((32, ROWS, 128), F32)],
        compiler_params=pltpu.CompilerParams(vmem_limit_bytes=32 * MIB),
        name="pack",
    )(jnp.asarray(_pack_matrix(), BF), flat)

    messages, swapped = lax.optimization_barrier((messages, swapped))
    pair = jnp.stack([weights, swapped])
    def swap(piece):
        return lax.ppermute(piece, "core", [(0, 1), (1, 0)])

    right = lax.ppermute(pair, "x", [(i, (i - 1) % 4) for i in range(4)])
    left = lax.ppermute(pair, "x", [(i, (i + 1) % 4) for i in range(4)])
    picked = pl.pallas_call(
        _pick_kernel,
        out_shape=jax.ShapeDtypeStruct(pair.shape, BF),
        in_specs=[pl.BlockSpec(memory_space=pltpu.SMEM)] + [pl.BlockSpec(memory_space=pltpu.VMEM)] * 2,
        cost_estimate=pl.CostEstimate(flops=PICK_FLOPS, bytes_accessed=1400000, transcendentals=0),
        name="pick",
    )(core.astype(jnp.int32).reshape(1), right, left)
    far = lax.ppermute(
        picked, ("core", "x"), [(c * 4 + i, c * 4 + (i - 1 + 2 * c) % 4) for c in range(2) for i in range(4)]
    )
    sides = jnp.stack([right, left])
    own = [pair, sides, far]
    other = [swap(piece) for piece in own]
    raw = lax.all_to_all(messages, ("zh", "y", "zl", "x"), 0, 0, tiled=True)
    partial = pl.pallas_call(
        _conv_kernel,
        out_shape=jax.ShapeDtypeStruct((64, ROWS, 128), BF),
        in_specs=[pl.BlockSpec(memory_space=pltpu.SMEM)]
        + [pl.BlockSpec(memory_space=pltpu.VMEM)] * 2
        + [pl.BlockSpec(memory_space=pl.ANY)] * 6,
        out_specs=pl.BlockSpec(memory_space=pltpu.VMEM),
        scratch_shapes=CONV_SCRATCH,
        compiler_params=pltpu.CompilerParams(vmem_limit_bytes=44 * MIB),
        name="conv",
    )(where, raw, branch_shift.reshape(1, 128), *own, *other)

    arrived = lax.all_to_all(partial, ("zh", "y", "zl", "x"), 0, 0, tiled=True)
    by_cols, by_samples = _unpack_matrices()
    classes = jnp.concatenate([class_weight.T, jnp.zeros((5, 256), BF)])
    projected, loss = pl.pallas_call(
        _final_kernel,
        out_shape=(jax.ShapeDtypeStruct((108, 2, 256), BF), jax.ShapeDtypeStruct((6, 2, 18), F32)),
        scratch_shapes=[pltpu.VMEM((16, ROWS + 8, 128), F32), pltpu.VMEM((256, 1024), BF)],
        compiler_params=pltpu.CompilerParams(vmem_limit_bytes=32 * MIB),
        name="final",
    )(
        arrived,
        proj_weight,
        classes,
        labels.transpose(1, 0, 2).reshape(1, 216),
        jnp.asarray(by_cols, BF),
        jnp.asarray(by_samples, BF),
    )
    return (
        projected.reshape(6, 18, 2, 256).transpose(2, 0, 1, 3),
        loss.transpose(1, 0, 2),
    )


def solution(mesh):
    fine = Mesh(mesh.devices.reshape(2, 4, 2, 2, 4), ("zh", "y", "core", "zl", "x"))
    tile, chan = ("zh", "y", "core"), ("zl", "x")
    return jax.shard_map(
        body,
        mesh=fine,
        in_specs=(
            P(None, tile, chan, None),
            P(None, None, None, tile, chan),
            P(tile, chan),
            P(None, chan),
            P(),
            P(),
            P(None, tile, chan),
        ),
        out_specs=(P(None, tile, chan, None), P(None, tile, chan)),
        check_vma=False,
    )
```
